256 devices in a mesh: dp: 4 (over y_hi, core), ctx: 64 (over z, y_lo, x).
Axes of the slice: x: 4, y: 4 (y_hi: 2, y_lo: 2; y = y_hi * 2 + y_lo), z: 8, core: 2. Of those that a mesh axis runs over, the one named last changes fastest.
Arguments:
- hidden_states: bfloat16 [4, 8192, 1024], P('dp', 'ctx'), may hold values from -8 to 8
- short_weight: float32 [2, 3, 1024], replicated, may hold values from -3 to 3
- long_filter: bfloat16 [2, 512, 8192], P(None, 'ctx'), may hold values from -4 to 4
- cotangent: bfloat16 [4, 8192, 1024], P('dp', 'ctx'), may hold values from -0.03125 to 0.03125
Outputs:
- mixer_output: bfloat16 [4, 8192, 1024], P('dp', 'ctx')
- grad_filter: float32 [2, 512, 8192], P(None, 'ctx')
- grad_short: float32 [2, 3, 2, 512], P(None, None, None, 'ctx')
The draws below stay inside these ranges and needn't reach their ends.
All inputs are finite; a program needn't handle non-finite values.
Results may differ from the reference program's by a relative error of at most 0.0057.
Values may be sent and summed in bfloat16 or wider, within the bound.
A program may use at most 64 MiB of HBM per device.

```python
import math
import jax
import jax.numpy as jnp
from jax import lax

D = 1024
TAPS = 3
L = 8192
BATCH = 4


def draw_hidden_states(key, part):
    base_key = jax.random.fold_in(key, 11)
    key_noise, key_rows, key_cols = jax.random.split(base_key, 3)
    low_log = math.log(0.3)
    high_log = math.log(3.0)
    noise_part = jax.random.normal(key_noise, (BATCH, L, D), jnp.float32)
    row_scale = jnp.exp(jax.random.uniform(key_rows, (BATCH, L, 1), jnp.float32, low_log, high_log))
    column_scale = jnp.exp(jax.random.uniform(key_cols, (1, 1, D), jnp.float32, low_log, high_log))
    return jnp.clip(noise_part * row_scale * column_scale, -8.0, 8.0).astype(jnp.bfloat16)


def draw_long_filter(key, part):
    base_key = jax.random.fold_in(key, 23)
    key_rates, key_noise = jax.random.split(base_key, 2)
    rows = D // 2
    decay_rates = jnp.exp(jax.random.uniform(key_rates, (2, rows, 1), jnp.float32, math.log(0.5), math.log(40.0)))
    noise_part = jnp.clip(jax.random.normal(key_noise, (2, rows, L), jnp.float32), -4.0, 4.0)
    positions = jnp.arange(L, dtype=jnp.float32) / L
    energy = (1.0 - jnp.exp(-2.0 * decay_rates)) / (1.0 - jnp.exp(-2.0 * decay_rates / L))
    shaped = noise_part * jnp.exp(-decay_rates * positions[None, None, :]) / jnp.sqrt(energy)
    return shaped.astype(jnp.bfloat16)


def block_levels(stream_key, extent, pieces, smallest, high):
    loudness = 1.0
    for position, blocks in pieces:
        heights = jax.random.uniform(jax.random.fold_in(jax.random.fold_in(stream_key, 6), position), (blocks,), jnp.float32, smallest / len(pieces), high / len(pieces))
        loudness = loudness * jnp.repeat(jnp.exp(heights), extent[position] // blocks).reshape((-1,) + (1,) * (len(extent) - 1 - position))
    return loudness


def normal_values(own_key, dims, width, bound, cuts=(), held_as=jnp.bfloat16):
    result = jax.random.normal(own_key, dims, jnp.float32) * width
    if len(cuts) > 0:
        result = block_levels(own_key, dims, cuts, -0.22, 0.18) * result
    return jnp.clip(result, min=-bound, max=bound).astype(held_as)


def setup_inputs(seed: int = 0) -> dict:
    key_list = jax.random.split(jax.random.key(seed), 5)
    hidden_states = draw_hidden_states(jax.random.fold_in(key_list[4], 71), 0)
    short_weight = normal_values(key_list[1], (2, TAPS, D), 0.6, 3.0, (), jnp.float32)
    long_filter = draw_long_filter(jax.random.fold_in(key_list[4], 71), 0)
    cotangent = normal_values(key_list[3], (BATCH, L, D), (1.0 / (BATCH * L) ** 0.5), 0.03125, ((0, 4), (1, 64)))
    return dict(hidden_states=hidden_states, short_weight=short_weight, long_filter=long_filter, cotangent=cotangent)


def delayed(field, offset):
    if offset == 0:
        return field
    padded = jnp.pad(field, ((0, 0), (offset, 0)))
    return padded[:, :field.shape[1]]

def spectrum(field):
    return jnp.fft.rfft(field, n=2 * field.shape[-1], axis=-1)

def restore(spec, length):
    return jnp.fft.irfft(spec, n=2 * length, axis=-1)[..., :length]

def strand(normed, upstream, tap_weights, filter_rows):
    length = normed.shape[1]
    tap_count = tap_weights.shape[1]
    shifted = [delayed(normed, offset) for offset in range(tap_count)]
    value_stream = jnp.zeros_like(normed)
    gate_stream = jnp.zeros_like(normed)
    for offset in range(tap_count):
        value_stream = value_stream + tap_weights[0, offset][:, None] * shifted[offset]
        gate_stream = gate_stream + tap_weights[1, offset][:, None] * shifted[offset]
    filter_spec = spectrum(filter_rows)
    value_spec = spectrum(value_stream)
    conv_stream = restore(filter_spec * value_spec, length)
    gated = gate_stream * conv_stream
    conv_grad = upstream * gate_stream
    gate_grad = upstream * conv_stream
    grad_spec = spectrum(conv_grad)
    value_grad = restore(jnp.conj(filter_spec) * grad_spec, length)
    filter_grad = restore(grad_spec * jnp.conj(value_spec), length)
    value_taps = jnp.stack([lax.optimization_barrier(jnp.sum(value_grad * shifted[offset], axis=1)) for offset in range(tap_count)])
    gate_taps = jnp.stack([lax.optimization_barrier(jnp.sum(gate_grad * shifted[offset], axis=1)) for offset in range(tap_count)])
    return (gated, filter_grad, jnp.stack([value_taps, gate_taps]))

def reference(hidden_states, short_weight, long_filter, cotangent):
    half = long_filter.shape[1]
    paired = long_filter.astype(jnp.float32)
    filter_rows = jnp.concatenate([paired[0], paired[1][::-1]], axis=0)
    reverse_rows = filter_rows[::-1]
    reverse_taps = short_weight[:, :, ::-1]

    def one_sequence(inputs):
        hidden_row, upstream = inputs
        values = hidden_row.astype(jnp.float32)
        row_scale = lax.rsqrt(lax.optimization_barrier(jnp.mean(values * values, axis=1, keepdims=True)) + 1e-06)
        rounded = (values * row_scale).astype(jnp.bfloat16)
        normed = lax.optimization_barrier(rounded).astype(jnp.float32).T
        upstream_rows = upstream.astype(jnp.float32).T
        forward_part = strand(normed, upstream_rows, short_weight, filter_rows)
        reverse_part = strand(normed[:, ::-1], upstream_rows[:, ::-1], reverse_taps, reverse_rows)
        mixed = (forward_part[0] + reverse_part[0][:, ::-1]).T.astype(jnp.bfloat16)
        filter_total = forward_part[1] + reverse_part[1][::-1]
        tap_total = forward_part[2] + reverse_part[2][:, :, ::-1]
        return (mixed, filter_total, tap_total)
    mixed, filter_parts, tap_parts = lax.map(one_sequence, (hidden_states, cotangent))
    full_filter = lax.optimization_barrier(jnp.sum(filter_parts, axis=0))
    full_taps = lax.optimization_barrier(jnp.sum(tap_parts, axis=0))
    grad_filter = jnp.stack([full_filter[:half], full_filter[::-1][:half]])
    grad_short = jnp.stack([full_taps[..., :half], full_taps[..., ::-1][..., :half]], axis=2)
    return (mixed, grad_filter, grad_short)
```

```python
import functools, math
import numpy as np, ml_dtypes
import jax, jax.numpy as jnp
from jax import lax
from jax.experimental import pallas as pl
from jax.experimental.pallas import tpu as pltpu

BF = jnp.bfloat16
F32 = jnp.float32
NB = 64
LN = 128
CH = 16


def split(x):
    hi = x.astype(ml_dtypes.bfloat16)
    lo = (x - hi.astype(np.float64)).astype(ml_dtypes.bfloat16)
    return hi, lo


def constants():
    n = 2 * NB * LN
    k1 = np.arange(NB)[:, None] + 0.5
    n1 = np.arange(NB)[None, :]
    th = 2 * np.pi * k1 * n1 / LN
    a = np.concatenate([np.cos(th), -np.sin(th)], 0)
    b = np.concatenate([np.cos(th.T), -np.sin(th.T)], 1) * (2.0 / n)
    tw = 2 * np.pi * k1 * np.arange(LN)[None, :] / n
    twc, tws = np.cos(tw), np.sin(tw)
    ph = 2 * np.pi * np.outer(np.arange(LN), np.arange(LN)) / LN
    c, s = np.cos(ph), np.sin(ph)
    m = np.block([[c, -s], [s, c]])
    mi = np.block([[c, s], [-s, c]])
    ah, al = split(a)
    bh, bl = split(b)
    mh, ml = split(m)
    ih, il = split(mi)
    amat = np.concatenate([ah, ah, al], 1)
    bmat = np.concatenate([bh, bl], 1)
    tws = np.stack([twc, tws]).astype(np.float32)
    mats = np.stack([mh, ml, ih, il])
    return amat, bmat, tws, mats


def dot(a, b):
    return jnp.dot(a, b, preferred_element_type=F32)


def hilo(x):
    hi = x.astype(BF)
    return hi, (x - hi.astype(F32)).astype(BF)


def row_f(f):
    return f if f < 8 else 23 - f


def rows_of(c):
    return pl.ds(c, NB, stride=CH)


def shift(x, k):
    m = x.shape[0] - 2
    lane = lax.broadcasted_iota(jnp.int32, (1, 1, LN), 2)
    if k == 0:
        return x[1:m + 1]
    if k > 0:
        r = pltpu.roll(x[0:m + 1], k, 2)
        return jnp.where(lane < k, r[0:m], r[1:m + 1])
    r = pltpu.roll(x[1:m + 2], LN + k, 2)
    return jnp.where(lane >= LN + k, r[1:m + 1], r[0:m])


def forward(src, spec, amat, tws, mats, zs, order, exact, precise):
    twc, tws_ = tws[0], tws[1]
    for pair in range(8):
        x = jnp.concatenate([src[rows_of(order[2 * pair]), :], src[rows_of(order[2 * pair + 1]), :]], 1)
        hi, lo = hilo(x)
        if exact:
            p = dot(amat[:, 64:192], jnp.concatenate([hi, hi], 0))
        else:
            p = dot(amat[...], jnp.concatenate([hi, lo, hi], 0))
        for h in range(2):
            re = p[0:64, h * LN:(h + 1) * LN]
            im = p[64:128, h * LN:(h + 1) * LN]
            z = jnp.concatenate([re * twc + im * tws_, im * twc - re * tws_], 1)
            zh, zl = hilo(z)
            r = (2 * pair + h) * NB
            zs[0, r:r + NB, :] = zh
            if precise > 1:
                zs[1, r:r + NB, :] = zl
    big(zs, spec, mats[0], mats[1], precise)


def big(zs, out, mh, ml, precise):
    for blk in range(4):
        rr = pl.ds(blk * 256, 256)
        zh = zs[0, rr, :]
        acc = dot(zh, mh)
        if precise > 0:
            acc = acc + dot(zh, ml)
        if precise > 1:
            acc = acc + dot(zs[1, rr, :], mh)
        out[rr, :] = acc


def put(zs, f, re, im, precise):
    z = jnp.concatenate([re, im], 1)
    zh, zl = hilo(z)
    zs[0, f * NB:(f + 1) * NB, :] = zh
    if precise > 1:
        zs[1, f * NB:(f + 1) * NB, :] = zl


def inverse(zs, tmp, dst, bmat, tws, mats, order, precise):
    big(zs, tmp, mats[2], mats[3], precise)
    twc, tws_ = tws[0], tws[1]
    for pair in range(8):
        us = []
        for h in range(2):
            r = (2 * pair + h) * NB
            re = tmp[r:r + NB, 0:LN]
            im = tmp[r:r + NB, LN:2 * LN]
            us.append(jnp.concatenate([re * twc - im * tws_, re * tws_ + im * twc], 0))
        u = jnp.concatenate(us, 1)
        uh, ul = hilo(u)
        y = dot(bmat[...], jnp.concatenate([uh, uh], 0))
        if precise > 1:
            y = y + dot(bmat[:, 0:128], ul)
        dst[rows_of(order[2 * pair]), :] = y[:, 0:LN]
        dst[rows_of(order[2 * pair + 1]), :] = y[:, LN:2 * LN]


def halves(ref, f):
    r = slice(f * NB, (f + 1) * NB)
    return ref[r, 0:LN], ref[r, LN:2 * LN]


def tap_rows(sw_ref, me, flipped, filter_order):
    row = lax.broadcasted_iota(jnp.int32, (CH, 1024), 0)
    lane = lax.broadcasted_iota(jnp.int32, (CH, 1024), 1)
    low = 8 * me + row
    if filter_order:
        high = 1023 - 8 * me - (row - 8)
    else:
        high = 1016 - 8 * me + (row - 8)
    chan = jnp.where(row < 8, low, high)
    if flipped:
        chan = 1023 - chan
    hit = lane == chan
    out = []
    for i in range(2):
        for k in range(3):
            w = sw_ref[i, k:k + 1, :]
            out.append(jnp.sum(jnp.where(hit, w, 0.0), axis=1, keepdims=True))
    return out


def wide(x):
    return jnp.broadcast_to(x, (CH, LN))[None]


STEP = 4
P_G, P_S, P_D, P_C, P_Q = 2, 1, 1, 1, 1

def kernel(recv, filt, sw, amat, bmat, tws, mats, out, gf, gs,
           xpad, fpad, qpad, buf, buf2, spec_s, spec_g, spec_d, tmp, zs):
    me = lax.axis_index("ctx")
    recv_order = list(range(CH))
    filt_order = list(range(CH))
    zero = jnp.zeros((CH, LN), F32)
    for p in (xpad, fpad, qpad):
        p[0] = zero
        p[NB + 1] = zero
    wf = [wide(w) for w in tap_rows(sw, me, False, True)]
    wn = [wide(w) for w in tap_rows(sw, me, False, False)]
    wr = [wide(w) for w in tap_rows(sw, me, True, False)]

    for i in range(NB):
        blk = filt[:, :, i * LN:(i + 1) * LN].astype(F32).reshape(CH, LN)
        fpad[i + 1] = blk

    def fold(i, _):
        x = fpad[pl.ds(i * STEP, STEP + 2)]
        g = wf[0] * shift(x, 0) + wf[1] * shift(x, 1) + wf[2] * shift(x, 2)
        buf[pl.ds(pl.multiple_of(i * STEP * CH, STEP * CH), STEP * CH), :] = g.reshape(STEP * CH, LN)
        return 0
    lax.fori_loop(0, NB // STEP, fold, 0)
    forward(buf, spec_g, amat, tws, mats, zs, filt_order, False, P_G)

    for i in range(NB):
        xpad[i + 1] = recv[i, 0:CH, :].astype(F32)
    xrows = xpad.reshape((NB + 2) * CH, LN)
    forward(xrows.at[pl.ds(CH, NB * CH)], spec_s, amat, tws, mats, zs, recv_order, True, P_S)

    for f in range(CH):
        r = row_f(f)
        gr, gi = halves(spec_g, f)
        sr, si = halves(spec_s, r)
        put(zs, r, gr * sr - gi * si, gr * si + gi * sr, P_C)
    inverse(zs, tmp, buf, bmat, tws, mats, recv_order, P_C)
    for f in range(CH):
        r = row_f(f)
        gr, gi = halves(spec_g, f)
        sr, si = halves(spec_s, 15 - r)
        put(zs, 15 - r, gr * sr + gi * si, gr * si - gi * sr, P_C)
    inverse(zs, tmp, buf2, bmat, tws, mats, recv_order, P_C)

    def gates(i, acc):
        x = xpad[pl.ds(i * STEP, STEP + 2)]
        xs = {k: shift(x, k) for k in range(-2, 3)}
        rr = pl.ds(pl.multiple_of(i * STEP * CH, STEP * CH), STEP * CH)
        cf = buf[rr, :].reshape(STEP, CH, LN)
        cr = buf2[rr, :].reshape(STEP, CH, LN)
        gatef = wn[3] * xs[0] + wn[4] * xs[1] + wn[5] * xs[2]
        gater = wr[3] * xs[0] + wr[4] * xs[-1] + wr[5] * xs[-2]
        mix = gatef * cf + gater * cr
        ct = recv[pl.ds(i * STEP, STEP), CH:2 * CH, :].astype(F32)
        out[pl.ds(i * STEP, STEP)] = mix.astype(BF)
        buf[rr, :] = (ct * gatef).reshape(STEP * CH, LN)
        buf2[rr, :] = (ct * gater).reshape(STEP * CH, LN)
        cf = cf * ct
        cr = cr * ct
        new = [jnp.sum(cf * xs[k], 0) for k in range(3)] + [jnp.sum(cr * xs[-k], 0) for k in range(3)]
        return tuple(a + b for a, b in zip(acc, new))
    acc = lax.fori_loop(0, NB // STEP, gates, (zero,) * 6)
    a_sum = [jnp.sum(a, 1, keepdims=True) for a in acc]

    forward(buf, spec_d, amat, tws, mats, zs, recv_order, False, P_D)
    forward(buf2, spec_g, amat, tws, mats, zs, recv_order, False, P_D)
    for f in range(CH):
        r = row_f(f)
        dr, di = halves(spec_d, r)
        sr, si = halves(spec_s, r)
        er, ei = halves(spec_g, 15 - r)
        tr, ti = halves(spec_s, 15 - r)
        put(zs, f, dr * sr + di * si + er * tr + ei * ti, di * sr - dr * si + er * ti - ei * tr, P_Q)
    inverse(zs, tmp, qpad.reshape((NB + 2) * CH, LN).at[pl.ds(CH, NB * CH)], bmat, tws, mats, filt_order, P_Q)

    def grads(i, acc):
        q = qpad[pl.ds(i * STEP, STEP + 2)]
        qs = [shift(q, -k) for k in range(3)]
        rr = pl.ds(pl.multiple_of(i * STEP * CH, STEP * CH), STEP * CH)
        fl = fpad[pl.ds(i * STEP + 1, STEP)]
        g = wf[0] * qs[0] + wf[1] * qs[1] + wf[2] * qs[2]
        buf[rr, :] = g.reshape(STEP * CH, LN)
        return tuple(a + jnp.sum(fl * qs[k], 0) for k, a in enumerate(acc))
    acc = lax.fori_loop(0, NB // STEP, grads, (zero,) * 3)
    for i in range(NB):
        gf[:, :, i * LN:(i + 1) * LN] = buf[i * CH:(i + 1) * CH, :].reshape(2, 8, LN)
    s0 = [jnp.sum(a, 1, keepdims=True) for a in acc]
    for k in range(3):
        gs[k] = jnp.broadcast_to(s0[k], (CH, LN))
        gs[3 + k] = jnp.broadcast_to(a_sum[k], (CH, LN))
        gs[6 + k] = jnp.broadcast_to(a_sum[3 + k], (CH, LN))


def run_kernel(recv, filt, sw):
    amat, bmat, tws, mats = constants()
    vm = pl.BlockSpec(memory_space=pltpu.VMEM)
    return pl.pallas_call(
        kernel,
        out_shape=(
            jax.ShapeDtypeStruct((NB, CH, LN), BF),
            jax.ShapeDtypeStruct((2, 8, NB * LN), F32),
            jax.ShapeDtypeStruct((9, CH, LN), F32),
        ),
        in_specs=[vm] * 7,
        out_specs=(vm,) * 3,
        scratch_shapes=[
            pltpu.VMEM((NB + 2, CH, LN), F32),
            pltpu.VMEM((NB + 2, CH, LN), F32),
            pltpu.VMEM((NB + 2, CH, LN), F32),
            pltpu.VMEM((NB * CH, LN), F32),
            pltpu.VMEM((NB * CH, LN), F32),
            pltpu.VMEM((CH * NB, 2 * LN), F32),
            pltpu.VMEM((CH * NB, 2 * LN), F32),
            pltpu.VMEM((CH * NB, 2 * LN), F32),
            pltpu.VMEM((CH * NB, 2 * LN), F32),
            pltpu.VMEM((2, CH * NB, 2 * LN), BF),
        ],
        compiler_params=pltpu.CompilerParams(vmem_limit_bytes=48 << 20),
    )(recv, filt, sw, jnp.asarray(amat), jnp.asarray(bmat), jnp.asarray(tws), jnp.asarray(mats))


def local(hidden, sw, filt, cot):
    x = hidden[0].astype(F32)
    scale = lax.rsqrt(jnp.mean(x * x, axis=1, keepdims=True) + 1e-06)
    normed = (x * scale).astype(BF)

    def chunk(a):
        a = a.T.reshape(128, 8, LN)
        return jnp.stack([a[:NB], a[NB:][::-1]], 1).reshape(NB, CH, LN)
    send = jnp.concatenate([chunk(normed), chunk(cot[0])], 1)
    recv = lax.all_to_all(send, "ctx", 0, 0, tiled=True)
    out, gf, gs = run_kernel(recv, filt, sw)
    back = lax.all_to_all(out, "ctx", 0, 0, tiled=True)
    back = back.reshape(NB, 2, 8, LN)
    chan = jnp.concatenate([back[:, 0].reshape(512, LN), back[::-1, 1].reshape(512, LN)], 0)
    gs = gs[:, :, 0].reshape(3, 3, CH)
    s0 = gs[0].reshape(3, 2, 8)
    a, b = gs[1], gs[2]
    s1 = jnp.stack([a[:, :8] + b[:, ::-1][:, :8], a[:, ::-1][:, :8] + b[:, :8]], 1)
    gf, gs = lax.psum((gf, jnp.stack([s0, s1])), "dp")
    return chan.T[None], gf, gs


def solution(mesh):
    from jax.sharding import PartitionSpec as P
    in_specs = (P("dp", "ctx", None), P(), P(None, "ctx", None), P("dp", "ctx", None))
    out_specs = (P("dp", "ctx", None), P(None, "ctx", None), P(None, None, None, "ctx"))
    return jax.shard_map(local, mesh=mesh, in_specs=in_specs, out_specs=out_specs, check_vma=False)
```

```python
import numpy as np, ml_dtypes
import jax, jax.numpy as jnp
from jax import lax
from jax.experimental import pallas as pl
from jax.experimental.pallas import tpu as pltpu
from jax.sharding import PartitionSpec as P

BF = jnp.bfloat16
F32 = jnp.float32
NB = 64
LN = 128
CH = 16


def split(x):
    hi = x.astype(ml_dtypes.bfloat16)
    lo = (x - hi.astype(np.float64)).astype(ml_dtypes.bfloat16)
    return hi, lo


def constants():
    n = 2 * NB * LN
    k1 = np.arange(NB)[:, None] + 0.5
    n1 = np.arange(NB)[None, :]
    th = 2 * np.pi * k1 * n1 / LN
    a = np.concatenate([np.cos(th), -np.sin(th)], 0)
    b = np.concatenate([np.cos(th.T), -np.sin(th.T)], 1) * (2.0 / n)
    tw = 2 * np.pi * k1 * np.arange(LN)[None, :] / n
    twc, tws = np.cos(tw), np.sin(tw)
    ph = 2 * np.pi * np.outer(np.arange(LN), np.arange(LN)) / LN
    c, s = np.cos(ph), np.sin(ph)
    m = np.block([[c, -s], [s, c]])
    mi = np.block([[c, s], [-s, c]])
    ah, al = split(a)
    bh, bl = split(b)
    mh, ml = split(m)
    ih, il = split(mi)
    amat = np.concatenate([ah, ah, al], 1)
    bmat = np.concatenate([bh, bl], 1)
    tws = np.stack([twc, tws]).astype(np.float32)
    mats = np.stack([mh, ml, ih, il])
    return amat, bmat, tws, mats


def dot(a, b):
    return jnp.dot(a, b, preferred_element_type=F32)


def hilo(x):
    hi = x.astype(BF)
    return hi, (x - hi.astype(F32)).astype(BF)


def row_f(f):
    return f if f < 8 else 23 - f


def rows_of(c):
    return pl.ds(c, NB, stride=CH)


def shift(x, k):
    m = x.shape[0] - 2
    lane = lax.broadcasted_iota(jnp.int32, (1, 1, LN), 2)
    if k == 0:
        return x[1:m + 1]
    if k > 0:
        r = pltpu.roll(x[0:m + 1], k, 2)
        return jnp.where(lane < k, r[0:m], r[1:m + 1])
    r = pltpu.roll(x[1:m + 2], LN + k, 2)
    return jnp.where(lane >= LN + k, r[1:m + 1], r[0:m])


def forward(src, spec, amat, tws, mats, zs, order, exact, precise):
    twc, tws_ = tws[0], tws[1]
    for pair in range(8):
        x = jnp.concatenate([src[rows_of(order[2 * pair]), :], src[rows_of(order[2 * pair + 1]), :]], 1)
        hi, lo = hilo(x)
        if exact:
            p = dot(amat[:, 64:192], jnp.concatenate([hi, hi], 0))
        else:
            p = dot(amat[...], jnp.concatenate([hi, lo, hi], 0))
        for h in range(2):
            re = p[0:64, h * LN:(h + 1) * LN]
            im = p[64:128, h * LN:(h + 1) * LN]
            z = jnp.concatenate([re * twc + im * tws_, im * twc - re * tws_], 1)
            zh, zl = hilo(z)
            r = (2 * pair + h) * NB
            zs[0, r:r + NB, :] = zh
            if precise > 1:
                zs[1, r:r + NB, :] = zl
    big(zs, spec, mats[0], mats[1], precise)


def big(zs, out, mh, ml, precise):
    for blk in range(4):
        rr = pl.ds(blk * 256, 256)
        zh = zs[0, rr, :]
        acc = dot(zh, mh)
        if precise > 0:
            acc = acc + dot(zh, ml)
        if precise > 1:
            acc = acc + dot(zs[1, rr, :], mh)
        out[rr, :] = acc


def put(zs, f, re, im, precise):
    z = jnp.concatenate([re, im], 1)
    zh, zl = hilo(z)
    zs[0, f * NB:(f + 1) * NB, :] = zh
    if precise > 1:
        zs[1, f * NB:(f + 1) * NB, :] = zl


def inverse(zs, tmp, dst, bmat, tws, mats, order, precise):
    big(zs, tmp, mats[2], mats[3], precise)
    twc, tws_ = tws[0], tws[1]
    for pair in range(8):
        us = []
        for h in range(2):
            r = (2 * pair + h) * NB
            re = tmp[r:r + NB, 0:LN]
            im = tmp[r:r + NB, LN:2 * LN]
            us.append(jnp.concatenate([re * twc - im * tws_, re * tws_ + im * twc], 0))
        u = jnp.concatenate(us, 1)
        uh, ul = hilo(u)
        y = dot(bmat[...], jnp.concatenate([uh, uh], 0))
        if precise > 1:
            y = y + dot(bmat[:, 0:128], ul)
        dst[rows_of(order[2 * pair]), :] = y[:, 0:LN]
        dst[rows_of(order[2 * pair + 1]), :] = y[:, LN:2 * LN]


def halves(ref, f):
    r = slice(f * NB, (f + 1) * NB)
    return ref[r, 0:LN], ref[r, LN:2 * LN]


def tap_rows(sw_ref, me, flipped, filter_order):
    row = lax.broadcasted_iota(jnp.int32, (CH, 1024), 0)
    lane = lax.broadcasted_iota(jnp.int32, (CH, 1024), 1)
    low = 8 * me + row
    if filter_order:
        high = 1023 - 8 * me - (row - 8)
    else:
        high = 1016 - 8 * me + (row - 8)
    chan = jnp.where(row < 8, low, high)
    if flipped:
        chan = 1023 - chan
    hit = lane == chan
    out = []
    for i in range(2):
        for k in range(3):
            w = sw_ref[i, k:k + 1, :]
            out.append(jnp.sum(jnp.where(hit, w, 0.0), axis=1, keepdims=True))
    return out


def wide(x):
    return jnp.broadcast_to(x, (CH, LN))[None]


STEP = 4
P_G, P_S, P_D, P_C, P_Q = 2, 1, 1, 1, 1
MESH = pl.DeviceIdType.MESH


def scatter(src, dst, send, recv):
    me = lax.axis_index("ctx")

    def one(o, _):
        q = lax.rem(me + o, NB)
        pltpu.make_async_remote_copy(
            src_ref=src.at[q], dst_ref=dst.at[me], send_sem=send, recv_sem=recv,
            device_id={"ctx": q}, device_id_type=MESH).start()
        return 0
    lax.fori_loop(1, NB, one, 0)
    dst[me] = src[me]


def await_all(ref, sem):
    part = ref.at[pl.ds(0, NB - 1)]
    pltpu.make_async_copy(part, part, sem).wait()


def to_chunks(get, dst):
    for j in range(4):
        low = get(j).T
        high = get(7 - j).T
        for g in range(16):
            both = jnp.concatenate([low[8 * g:8 * g + 8], high[120 - 8 * g:128 - 8 * g]], 0)
            dst[16 * j + g] = both.astype(BF)


def kernel(hid, cot, filt, sw, amat, bmat, tws, mats, mixed, gf, gs,
           sendx, sendc, recvx, recvc, sendo, recvo,
           xpad, fpad, qpad, buf, buf2, spec_s, spec_g, spec_d, tmp, zs,
           half_out, half_in, pair_out, pair_in, small_in,
           sx, rx, sc, rc, so, ro, s2, r2):
    me = lax.axis_index("ctx")
    dp = lax.axis_index("dp")
    core = lax.rem(dp, 2)
    yhi = dp // 2
    mate = yhi * 2 + 1 - core
    far = (1 - yhi) * 2 + core
    barrier = pltpu.get_barrier_semaphore()

    def greet(o, _):
        pl.semaphore_signal(barrier, inc=1, device_id={"ctx": lax.rem(me + o, NB)}, device_id_type=MESH)
        return 0
    lax.fori_loop(1, NB, greet, 0)
    for o in range(1, 4):
        pl.semaphore_signal(barrier, inc=1, device_id={"dp": lax.rem(dp + o, 4)}, device_id_type=MESH)

    recv_order = list(range(CH))
    filt_order = list(range(CH))
    zero = jnp.zeros((CH, LN), F32)
    for p in (xpad, fpad, qpad):
        p[0] = zero
        p[NB + 1] = zero

    x = hid[...].astype(F32)
    scale = lax.rsqrt(jnp.mean(x * x, axis=1, keepdims=True) + 1e-06)
    to_chunks(lambda j: hid[:, j * LN:(j + 1) * LN].astype(F32) * scale, sendx)
    pl.semaphore_wait(barrier, NB - 1 + 3)
    scatter(sendx, recvx, sx, rx)
    to_chunks(lambda j: cot[:, j * LN:(j + 1) * LN].astype(F32), sendc)
    scatter(sendc, recvc, sc, rc)

    wf = [wide(w) for w in tap_rows(sw, me, False, True)]
    wn = [wide(w) for w in tap_rows(sw, me, False, False)]
    wr = [wide(w) for w in tap_rows(sw, me, True, False)]

    for i in range(NB):
        fpad[i + 1] = filt[:, :, i * LN:(i + 1) * LN].astype(F32).reshape(CH, LN)

    def rows(i):
        return pl.ds(pl.multiple_of(i * STEP * CH, STEP * CH), STEP * CH)

    def fold(i, _):
        v = fpad[pl.ds(i * STEP, STEP + 2)]
        g = wf[0] * shift(v, 0) + wf[1] * shift(v, 1) + wf[2] * shift(v, 2)
        buf[rows(i), :] = g.reshape(STEP * CH, LN)
        return 0
    lax.fori_loop(0, NB // STEP, fold, 0)
    forward(buf, spec_g, amat, tws, mats, zs, filt_order, False, P_G)

    await_all(recvx, rx)
    for i in range(NB):
        v = recvx[i].astype(F32)
        xpad[i + 1] = v
        buf[i * CH:(i + 1) * CH, :] = v
    forward(buf, spec_s, amat, tws, mats, zs, recv_order, True, P_S)

    for f in range(CH):
        r = row_f(f)
        gr, gi = halves(spec_g, f)
        sr, si = halves(spec_s, r)
        put(zs, r, gr * sr - gi * si, gr * si + gi * sr, P_C)
    inverse(zs, tmp, buf, bmat, tws, mats, recv_order, P_C)
    for f in range(CH):
        r = row_f(f)
        gr, gi = halves(spec_g, f)
        sr, si = halves(spec_s, 15 - r)
        put(zs, 15 - r, gr * sr + gi * si, gr * si - gi * sr, P_C)
    inverse(zs, tmp, buf2, bmat, tws, mats, recv_order, P_C)

    def mix(i, _):
        v = xpad[pl.ds(i * STEP, STEP + 2)]
        cf = buf[rows(i), :].reshape(STEP, CH, LN)
        cr = buf2[rows(i), :].reshape(STEP, CH, LN)
        gatef = wn[3] * shift(v, 0) + wn[4] * shift(v, 1) + wn[5] * shift(v, 2)
        gater = wr[3] * shift(v, 0) + wr[4] * shift(v, -1) + wr[5] * shift(v, -2)
        sendo[pl.ds(i * STEP, STEP)] = (gatef * cf + gater * cr).astype(BF)
        return 0
    lax.fori_loop(0, NB // STEP, mix, 0)
    scatter(sendo, recvo, so, ro)

    await_all(recvc, rc)

    def gates(i, acc):
        v = xpad[pl.ds(i * STEP, STEP + 2)]
        xs = {k: shift(v, k) for k in range(-2, 3)}
        ct = recvc[pl.ds(i * STEP, STEP)].astype(F32)
        cf = buf[rows(i), :].reshape(STEP, CH, LN) * ct
        cr = buf2[rows(i), :].reshape(STEP, CH, LN) * ct
        gatef = wn[3] * xs[0] + wn[4] * xs[1] + wn[5] * xs[2]
        gater = wr[3] * xs[0] + wr[4] * xs[-1] + wr[5] * xs[-2]
        buf[rows(i), :] = (ct * gatef).reshape(STEP * CH, LN)
        buf2[rows(i), :] = (ct * gater).reshape(STEP * CH, LN)
        new = [jnp.sum(cf * xs[k], 0) for k in range(3)] + [jnp.sum(cr * xs[-k], 0) for k in range(3)]
        return tuple(a + b for a, b in zip(acc, new))
    a_acc = lax.fori_loop(0, NB // STEP, gates, (zero,) * 6)

    forward(buf, spec_d, amat, tws, mats, zs, recv_order, False, P_D)
    forward(buf2, spec_g, amat, tws, mats, zs, recv_order, False, P_D)
    for f in range(CH):
        r = row_f(f)
        dr, di = halves(spec_d, r)
        sr, si = halves(spec_s, r)
        er, ei = halves(spec_g, 15 - r)
        tr, ti = halves(spec_s, 15 - r)
        put(zs, f, dr * sr + di * si + er * tr + ei * ti, di * sr - dr * si + er * ti - ei * tr, P_Q)
    inverse(zs, tmp, buf, bmat, tws, mats, filt_order, P_Q)
    for i in range(NB):
        qpad[i + 1] = buf[i * CH:(i + 1) * CH, :]

    def grads(i, acc):
        v = qpad[pl.ds(i * STEP, STEP + 2)]
        qs = [shift(v, -k) for k in range(3)]
        fl = fpad[pl.ds(i * STEP + 1, STEP)]
        g = wf[0] * qs[0] + wf[1] * qs[1] + wf[2] * qs[2]
        half_out[0, pl.ds(i * STEP, STEP)] = g[:, 0:8]
        half_out[1, pl.ds(i * STEP, STEP)] = g[:, 8:16]
        return tuple(a + jnp.sum(fl * qs[k], 0) for k, a in enumerate(acc))
    q_acc = lax.fori_loop(0, NB // STEP, grads, (zero,) * 3)

    first = pltpu.make_async_remote_copy(
        src_ref=half_out.at[1 - core], dst_ref=half_in, send_sem=s2.at[0], recv_sem=r2.at[0],
        device_id={"dp": mate}, device_id_type=MESH)
    first.start()
    lane = lax.broadcasted_iota(jnp.int32, (CH, LN), 1)
    small = zero
    for k, a in enumerate(q_acc + a_acc):
        small = jnp.where(lane == k, jnp.sum(a, 1, keepdims=True), small)
    small_in[dp] = small
    smalls = []
    for o in range(1, 4):
        c = pltpu.make_async_remote_copy(
            src_ref=small_in.at[dp], dst_ref=small_in.at[dp], send_sem=s2.at[2 + o], recv_sem=r2.at[2 + o],
            device_id={"dp": lax.rem(dp + o, 4)}, device_id_type=MESH)
        c.start()
        smalls.append(c)
    first.wait()
    for i in range(NB // 2):
        a = half_out[core, 2 * i:2 * i + 2] + half_in[2 * i:2 * i + 2]
        pair_out[i] = a.reshape(CH, LN).astype(BF)
    second = pltpu.make_async_remote_copy(
        src_ref=pair_out, dst_ref=pair_in, send_sem=s2.at[1], recv_sem=r2.at[1],
        device_id={"dp": far}, device_id_type=MESH)
    second.start()

    await_all(recvo, ro)
    for j in range(4):
        low = jnp.concatenate([recvo[16 * j + g].astype(F32)[0:8] for g in range(16)], 0)
        high = jnp.concatenate([recvo[16 * j + 15 - g].astype(F32)[8:16] for g in range(16)], 0)
        mixed[:, j * LN:(j + 1) * LN] = low.T.astype(BF)
        mixed[:, (7 - j) * LN:(8 - j) * LN] = high.T.astype(BF)

    second.wait()
    for i in range(NB // 2):
        t = pair_out[i].astype(F32) + pair_in[i].astype(F32)
        gf[core, :, 2 * i * LN:(2 * i + 1) * LN] = t[0:8]
        gf[core, :, (2 * i + 1) * LN:(2 * i + 2) * LN] = t[8:16]
    third = pltpu.make_async_remote_copy(
        src_ref=gf.at[core], dst_ref=gf.at[core], send_sem=s2.at[2], recv_sem=r2.at[2],
        device_id={"dp": mate}, device_id_type=MESH)
    third.start()
    for c in smalls:
        c.wait()
    gs[...] = (small_in[0] + small_in[1]) + (small_in[2] + small_in[3])
    await_all(sendx, sx)
    await_all(sendc, sc)
    await_all(sendo, so)
    third.wait()


def run_kernel(hid, cot, filt, sw):
    amat, bmat, tws, mats = constants()
    vm = pl.BlockSpec(memory_space=pltpu.VMEM)
    dma = pltpu.SemaphoreType.DMA
    chunks = pltpu.VMEM((NB, CH, LN), BF)
    padded = pltpu.VMEM((NB + 2, CH, LN), F32)
    flat = pltpu.VMEM((NB * CH, LN), F32)
    spec = pltpu.VMEM((CH * NB, 2 * LN), F32)
    return pl.pallas_call(
        kernel,
        out_shape=(
            jax.ShapeDtypeStruct((LN, 1024), BF),
            jax.ShapeDtypeStruct((2, 8, NB * LN), F32),
            jax.ShapeDtypeStruct((CH, LN), F32),
        ),
        in_specs=[vm] * 8,
        out_specs=(vm,) * 3,
        scratch_shapes=[chunks] * 6 + [padded] * 3 + [flat] * 2 + [spec] * 4 + [
            pltpu.VMEM((2, CH * NB, 2 * LN), BF),
            pltpu.VMEM((2, NB, 8, LN), F32),
            pltpu.VMEM((NB, 8, LN), F32),
            pltpu.VMEM((NB // 2, CH, LN), BF),
            pltpu.VMEM((NB // 2, CH, LN), BF),
            pltpu.VMEM((4, CH, LN), F32),
            dma, dma, dma, dma, dma, dma, dma((6,)), dma((6,)),
        ],
        compiler_params=pltpu.CompilerParams(
            vmem_limit_bytes=48 << 20, collective_id=0, has_side_effects=True),
    )(hid, cot, filt, sw, jnp.asarray(amat), jnp.asarray(bmat), jnp.asarray(tws), jnp.asarray(mats))


def local(hidden, sw, filt, cot):
    mixed, gf, gs = run_kernel(hidden[0], cot[0], filt, sw)
    gs = gs[:, :9].T.reshape(3, 3, CH)
    a, b = gs[1], gs[2]
    s0 = gs[0].reshape(3, 2, 8)
    s1 = jnp.stack([a[:, :8] + b[:, ::-1][:, :8], a[:, ::-1][:, :8] + b[:, :8]], 1)
    return mixed[None], gf, jnp.stack([s0, s1])


def solution(mesh):
    in_specs = (P("dp", "ctx", None), P(), P(None, "ctx", None), P("dp", "ctx", None))
    out_specs = (P("dp", "ctx", None), P(None, "ctx", None), P(None, None, None, "ctx"))
    return jax.shard_map(local, mesh=mesh, in_specs=in_specs, out_specs=out_specs, check_vma=False)
```

```python
import numpy as np, ml_dtypes
import jax, jax.numpy as jnp
from jax import lax
from jax.experimental import pallas as pl
from jax.experimental.pallas import tpu as pltpu
from jax.sharding import PartitionSpec as P

BF = jnp.bfloat16
F32 = jnp.float32
NB = 64
LN = 128
CH = 16


def split(x):
    hi = x.astype(ml_dtypes.bfloat16)
    lo = (x - hi.astype(np.float64)).astype(ml_dtypes.bfloat16)
    return hi, lo


def constants():
    n = 2 * NB * LN
    k1 = np.arange(NB)[:, None] + 0.5
    n1 = np.arange(NB)[None, :]
    th = 2 * np.pi * k1 * n1 / LN
    a = np.concatenate([np.cos(th), -np.sin(th)], 0)
    b = np.concatenate([np.cos(th.T), -np.sin(th.T)], 1) * (2.0 / n)
    tw = 2 * np.pi * k1 * np.arange(LN)[None, :] / n
    twc, tws = np.cos(tw), np.sin(tw)
    ph = 2 * np.pi * np.outer(np.arange(LN), np.arange(LN)) / LN
    c, s = np.cos(ph), np.sin(ph)
    m = np.block([[c, -s], [s, c]])
    mi = np.block([[c, s], [-s, c]])
    ah, al = split(a)
    bh, bl = split(b)
    mh, ml = split(m)
    ih, il = split(mi)
    amat = np.concatenate([ah, ah, al], 1)
    bmat = np.concatenate([bh, bl], 1)
    tws = np.stack([twc, tws]).astype(np.float32)
    mats = np.stack([mh, ml, ih, il])
    return amat, bmat, tws, mats


def dot(a, b):
    return jnp.dot(a, b, preferred_element_type=F32)


def hilo(x):
    hi = x.astype(BF)
    return hi, (x - hi.astype(F32)).astype(BF)


def row_f(f):
    return f if f < 8 else 23 - f


def rows_of(c):
    return pl.ds(c, NB, stride=CH)


def shift(x, k):
    m = x.shape[0] - 2
    lane = lax.broadcasted_iota(jnp.int32, (1, 1, LN), 2)
    if k == 0:
        return x[1:m + 1]
    if k > 0:
        r = pltpu.roll(x[0:m + 1], k, 2)
        return jnp.where(lane < k, r[0:m], r[1:m + 1])
    r = pltpu.roll(x[1:m + 2], LN + k, 2)
    return jnp.where(lane >= LN + k, r[1:m + 1], r[0:m])


def forward(src, spec, amat, tws, mats, zs, order, exact, precise):
    twc, tws_ = tws[0], tws[1]
    for pair in range(8):
        x = jnp.concatenate([src[rows_of(order[2 * pair]), :], src[rows_of(order[2 * pair + 1]), :]], 1)
        hi, lo = hilo(x)
        if exact:
            p = dot(amat[:, 64:192], jnp.concatenate([hi, hi], 0))
        else:
            p = dot(amat[...], jnp.concatenate([hi, lo, hi], 0))
        for h in range(2):
            re = p[0:64, h * LN:(h + 1) * LN]
            im = p[64:128, h * LN:(h + 1) * LN]
            z = jnp.concatenate([re * twc + im * tws_, im * twc - re * tws_], 1)
            zh, zl = hilo(z)
            r = (2 * pair + h) * NB
            zs[0, r:r + NB, :] = zh
            if precise > 1:
                zs[1, r:r + NB, :] = zl
    big(zs, spec, mats[0], mats[1], precise)


def big(zs, out, mh, ml, precise):
    for blk in range(4):
        rr = pl.ds(blk * 256, 256)
        zh = zs[0, rr, :]
        acc = dot(zh, mh)
        if precise > 0:
            acc = acc + dot(zh, ml)
        if precise > 1:
            acc = acc + dot(zs[1, rr, :], mh)
        out[rr, :] = acc


def put(zs, f, re, im, precise):
    z = jnp.concatenate([re, im], 1)
    zh, zl = hilo(z)
    zs[0, f * NB:(f + 1) * NB, :] = zh
    if precise > 1:
        zs[1, f * NB:(f + 1) * NB, :] = zl


def inverse(zs, tmp, dst, bmat, tws, mats, order, precise):
    big(zs, tmp, mats[2], mats[3], precise)
    twc, tws_ = tws[0], tws[1]
    for pair in range(8):
        us = []
        for h in range(2):
            r = (2 * pair + h) * NB
            re = tmp[r:r + NB, 0:LN]
            im = tmp[r:r + NB, LN:2 * LN]
            us.append(jnp.concatenate([re * twc - im * tws_, re * tws_ + im * twc], 0))
        u = jnp.concatenate(us, 1)
        uh, ul = hilo(u)
        y = dot(bmat[...], jnp.concatenate([uh, uh], 0))
        if precise > 1:
            y = y + dot(bmat[:, 0:128], ul)
        dst[rows_of(order[2 * pair]), :] = y[:, 0:LN]
        dst[rows_of(order[2 * pair + 1]), :] = y[:, LN:2 * LN]


def halves(ref, f):
    r = slice(f * NB, (f + 1) * NB)
    return ref[r, 0:LN], ref[r, LN:2 * LN]


def tap_rows(sw_ref, me, flipped, filter_order):
    row = lax.broadcasted_iota(jnp.int32, (CH, 1024), 0)
    lane = lax.broadcasted_iota(jnp.int32, (CH, 1024), 1)
    low = 8 * me + row
    if filter_order:
        high = 1023 - 8 * me - (row - 8)
    else:
        high = 1016 - 8 * me + (row - 8)
    chan = jnp.where(row < 8, low, high)
    if flipped:
        chan = 1023 - chan
    hit = lane == chan
    out = []
    for i in range(2):
        for k in range(3):
            w = sw_ref[k, i:i + 1, :]
            out.append(jnp.sum(jnp.where(hit, w, 0.0), axis=1, keepdims=True))
    return out


def wide(x):
    return jnp.broadcast_to(x, (CH, LN))[None]


STEP = 4
P_G, P_S, P_D, P_C, P_Q = 2, 1, 1, 1, 1
MESH = pl.DeviceIdType.MESH


def scatter(src, dst, send, recv):
    me = lax.axis_index("ctx")

    def one(o, _):
        q = lax.rem(me + o, NB)
        pltpu.make_async_remote_copy(
            src_ref=src.at[q], dst_ref=dst.at[me], send_sem=send, recv_sem=recv,
            device_id={"ctx": q}, device_id_type=MESH).start()
        return 0
    lax.fori_loop(1, NB, one, 0)
    dst[me] = src[me]


def await_all(ref, sem):
    part = ref.at[pl.ds(0, NB - 1)]
    pltpu.make_async_copy(part, part, sem).wait()


def to_chunks(get, dst):
    for j in range(4):
        low = get(j).T
        high = get(7 - j).T
        for g in range(16):
            both = jnp.concatenate([low[8 * g:8 * g + 8], high[120 - 8 * g:128 - 8 * g]], 0)
            dst[16 * j + g] = both.astype(BF)


def kernel(hid_h, cot_h, filt_h, sw_h, amat_h, bmat_h, tws_h, mats_h, mixed, gf, gs,
           hid, cot, filt, sw, amat, bmat, tws, mats,
           sendx, sendc, recvx, recvc, sendo, recvo,
           xpad, fpad, qpad, buf, buf2, spec_s, spec_g, spec_d, tmp, zs,
           half_out, half_in, pair_out, pair_in, small_in,
           sx, rx, sc, rc, so, ro, s2, r2, ins):
    pairs = ((hid_h, hid), (cot_h, cot), (filt_h, filt), (sw_h, sw), (amat_h, amat), (bmat_h, bmat), (tws_h, tws), (mats_h, mats))
    loads = [pltpu.make_async_copy(a, b, ins.at[i]) for i, (a, b) in enumerate(pairs)]
    for c in loads:
        c.start()
    me = lax.axis_index("ctx")
    dp = lax.axis_index("dp")
    core = lax.rem(dp, 2)
    yhi = dp // 2
    mate = yhi * 2 + 1 - core
    far = (1 - yhi) * 2 + core
    barrier = pltpu.get_barrier_semaphore()

    def greet(o, _):
        pl.semaphore_signal(barrier, inc=1, device_id={"ctx": lax.rem(me + o, NB)}, device_id_type=MESH)
        return 0
    lax.fori_loop(1, NB, greet, 0)
    for o in range(1, 4):
        pl.semaphore_signal(barrier, inc=1, device_id={"dp": lax.rem(dp + o, 4)}, device_id_type=MESH)

    recv_order = list(range(CH))
    filt_order = list(range(CH))
    zero = jnp.zeros((CH, LN), F32)
    for p in (xpad, fpad, qpad):
        p[0] = zero
        p[NB + 1] = zero

    loads[0].wait()
    x = hid[...].astype(F32)
    scale = lax.rsqrt(jnp.mean(x * x, axis=1, keepdims=True) + 1e-06)
    to_chunks(lambda j: hid[:, j * LN:(j + 1) * LN].astype(F32) * scale, sendx)
    pl.semaphore_wait(barrier, NB - 1 + 3)
    scatter(sendx, recvx, sx, rx)
    loads[1].wait()
    to_chunks(lambda j: cot[:, j * LN:(j + 1) * LN].astype(F32), sendc)
    scatter(sendc, recvc, sc, rc)

    for c in loads[2:]:
        c.wait()
    wf = [wide(w) for w in tap_rows(sw, me, False, True)]
    wn = [wide(w) for w in tap_rows(sw, me, False, False)]
    wr = [wide(w) for w in tap_rows(sw, me, True, False)]

    for i in range(NB):
        fpad[i + 1] = filt[:, :, i * LN:(i + 1) * LN].astype(F32).reshape(CH, LN)

    def rows(i):
        return pl.ds(pl.multiple_of(i * STEP * CH, STEP * CH), STEP * CH)

    def fold(i, _):
        v = fpad[pl.ds(i * STEP, STEP + 2)]
        g = wf[0] * shift(v, 0) + wf[1] * shift(v, 1) + wf[2] * shift(v, 2)
        buf[rows(i), :] = g.reshape(STEP * CH, LN)
        return 0
    lax.fori_loop(0, NB // STEP, fold, 0, unroll=NB // STEP)
    forward(buf, spec_g, amat, tws, mats, zs, filt_order, False, P_G)

    await_all(recvx, rx)
    for i in range(NB):
        v = recvx[i].astype(F32)
        xpad[i + 1] = v
        buf[i * CH:(i + 1) * CH, :] = v
    forward(buf, spec_s, amat, tws, mats, zs, recv_order, True, P_S)

    for f in range(CH):
        r = row_f(f)
        gr, gi = halves(spec_g, f)
        sr, si = halves(spec_s, r)
        put(zs, r, gr * sr - gi * si, gr * si + gi * sr, P_C)
    inverse(zs, tmp, buf, bmat, tws, mats, recv_order, P_C)
    for f in range(CH):
        r = row_f(f)
        gr, gi = halves(spec_g, f)
        sr, si = halves(spec_s, 15 - r)
        put(zs, 15 - r, gr * sr + gi * si, gr * si - gi * sr, P_C)
    inverse(zs, tmp, buf2, bmat, tws, mats, recv_order, P_C)

    def mix(i, _):
        v = xpad[pl.ds(i * STEP, STEP + 2)]
        cf = buf[rows(i), :].reshape(STEP, CH, LN)
        cr = buf2[rows(i), :].reshape(STEP, CH, LN)
        gatef = wn[3] * shift(v, 0) + wn[4] * shift(v, 1) + wn[5] * shift(v, 2)
        gater = wr[3] * shift(v, 0) + wr[4] * shift(v, -1) + wr[5] * shift(v, -2)
        sendo[pl.ds(i * STEP, STEP)] = (gatef * cf + gater * cr).astype(BF)
        return 0
    lax.fori_loop(0, NB // STEP, mix, 0, unroll=NB // STEP)
    scatter(sendo, recvo, so, ro)

    await_all(recvc, rc)

    def gates(i, acc):
        v = xpad[pl.ds(i * STEP, STEP + 2)]
        xs = {k: shift(v, k) for k in range(-2, 3)}
        ct = recvc[pl.ds(i * STEP, STEP)].astype(F32)
        cf = buf[rows(i), :].reshape(STEP, CH, LN) * ct
        cr = buf2[rows(i), :].reshape(STEP, CH, LN) * ct
        gatef = wn[3] * xs[0] + wn[4] * xs[1] + wn[5] * xs[2]
        gater = wr[3] * xs[0] + wr[4] * xs[-1] + wr[5] * xs[-2]
        buf[rows(i), :] = (ct * gatef).reshape(STEP * CH, LN)
        buf2[rows(i), :] = (ct * gater).reshape(STEP * CH, LN)
        new = [jnp.sum(cf * xs[k], 0) for k in range(3)] + [jnp.sum(cr * xs[-k], 0) for k in range(3)]
        return tuple(a + b for a, b in zip(acc, new))
    a_acc = lax.fori_loop(0, NB // STEP, gates, (zero,) * 6, unroll=NB // STEP)

    forward(buf, spec_d, amat, tws, mats, zs, recv_order, False, P_D)
    forward(buf2, spec_g, amat, tws, mats, zs, recv_order, False, P_D)
    for f in range(CH):
        r = row_f(f)
        dr, di = halves(spec_d, r)
        sr, si = halves(spec_s, r)
        er, ei = halves(spec_g, 15 - r)
        tr, ti = halves(spec_s, 15 - r)
        put(zs, f, dr * sr + di * si + er * tr + ei * ti, di * sr - dr * si + er * ti - ei * tr, P_Q)
    inverse(zs, tmp, buf, bmat, tws, mats, filt_order, P_Q)
    for i in range(NB):
        qpad[i + 1] = buf[i * CH:(i + 1) * CH, :]

    def grads(i, acc):
        v = qpad[pl.ds(i * STEP, STEP + 2)]
        qs = [shift(v, -k) for k in range(3)]
        fl = fpad[pl.ds(i * STEP + 1, STEP)]
        g = wf[0] * qs[0] + wf[1] * qs[1] + wf[2] * qs[2]
        half_out[0, pl.ds(i * STEP, STEP)] = g[:, 0:8]
        half_out[1, pl.ds(i * STEP, STEP)] = g[:, 8:16]
        return tuple(a + jnp.sum(fl * qs[k], 0) for k, a in enumerate(acc))
    q_acc = lax.fori_loop(0, NB // STEP, grads, (zero,) * 3, unroll=NB // STEP)

    first = pltpu.make_async_remote_copy(
        src_ref=half_out.at[1 - core], dst_ref=half_in, send_sem=s2.at[0], recv_sem=r2.at[0],
        device_id={"dp": mate}, device_id_type=MESH)
    first.start()
    lane = lax.broadcasted_iota(jnp.int32, (CH, LN), 1)
    small = zero
    for k, a in enumerate(q_acc + a_acc):
        small = jnp.where(lane == k, jnp.sum(a, 1, keepdims=True), small)
    small_in[dp] = small
    smalls = []
    for o in range(1, 4):
        c = pltpu.make_async_remote_copy(
            src_ref=small_in.at[dp], dst_ref=small_in.at[dp], send_sem=s2.at[2 + o], recv_sem=r2.at[2 + o],
            device_id={"dp": lax.rem(dp + o, 4)}, device_id_type=MESH)
        c.start()
        smalls.append(c)
    first.wait()
    for i in range(NB // 2):
        a = half_out[core, 2 * i:2 * i + 2] + half_in[2 * i:2 * i + 2]
        pair_out[i] = a.reshape(CH, LN).astype(BF)
    second = pltpu.make_async_remote_copy(
        src_ref=pair_out, dst_ref=pair_in, send_sem=s2.at[1], recv_sem=r2.at[1],
        device_id={"dp": far}, device_id_type=MESH)
    second.start()

    await_all(recvo, ro)
    for j in range(4):
        low = jnp.concatenate([recvo[16 * j + g].astype(F32)[0:8] for g in range(16)], 0)
        high = jnp.concatenate([recvo[16 * j + 15 - g].astype(F32)[8:16] for g in range(16)], 0)
        mixed[:, j * LN:(j + 1) * LN] = low.T.astype(BF)
        mixed[:, (7 - j) * LN:(8 - j) * LN] = high.T.astype(BF)

    second.wait()
    for i in range(NB // 2):
        t = pair_out[i].astype(F32) + pair_in[i].astype(F32)
        gf[core, :, 2 * i * LN:(2 * i + 1) * LN] = t[0:8]
        gf[core, :, (2 * i + 1) * LN:(2 * i + 2) * LN] = t[8:16]
    third = pltpu.make_async_remote_copy(
        src_ref=gf.at[core], dst_ref=gf.at[core], send_sem=s2.at[2], recv_sem=r2.at[2],
        device_id={"dp": mate}, device_id_type=MESH)
    third.start()
    for c in smalls:
        c.wait()
    total = (small_in[0] + small_in[1]) + (small_in[2] + small_in[3])
    row = lax.broadcasted_iota(jnp.int32, (CH, LN), 0)

    def flat_rows(item, target):
        return jnp.sum(jnp.where(row == target, total[:, item:item + 1], 0.0), 0, keepdims=True)[:, 0:8]
    for k in range(3):
        gs[0, k] = jnp.concatenate([flat_rows(k, lane), flat_rows(k, lane + 8)], 0)
        gs[1, k] = jnp.concatenate([
            flat_rows(3 + k, lane) + flat_rows(6 + k, 15 - lane),
            flat_rows(3 + k, 15 - lane) + flat_rows(6 + k, lane)], 0)
    await_all(sendx, sx)
    await_all(sendc, sc)
    await_all(sendo, so)
    third.wait()


def run_kernel(hid, cot, filt, sw):
    amat, bmat, tws, mats = constants()
    vm = pl.BlockSpec(memory_space=pltpu.VMEM)
    dma = pltpu.SemaphoreType.DMA
    chunks = pltpu.VMEM((NB, CH, LN), BF)
    padded = pltpu.VMEM((NB + 2, CH, LN), F32)
    flat = pltpu.VMEM((NB * CH, LN), F32)
    spec = pltpu.VMEM((CH * NB, 2 * LN), F32)
    ops = (hid, cot, filt, sw, jnp.asarray(amat), jnp.asarray(bmat), jnp.asarray(tws), jnp.asarray(mats))
    held = [pltpu.VMEM(a.shape, a.dtype) for a in ops]
    return pl.pallas_call(
        kernel,
        out_shape=(
            pltpu.VMEM((LN, 1024), BF),
            pltpu.VMEM((2, 8, NB * LN), F32),
            pltpu.VMEM((2, 3, 2, 8), F32),
        ),
        in_specs=[pl.BlockSpec(memory_space=pltpu.HBM)] * 8,
        out_specs=(vm,) * 3,
        scratch_shapes=held + [chunks] * 6 + [padded] * 3 + [flat] * 2 + [spec] * 4 + [
            pltpu.VMEM((2, CH * NB, 2 * LN), BF),
            pltpu.VMEM((2, NB, 8, LN), F32),
            pltpu.VMEM((NB, 8, LN), F32),
            pltpu.VMEM((NB // 2, CH, LN), BF),
            pltpu.VMEM((NB // 2, CH, LN), BF),
            pltpu.VMEM((4, CH, LN), F32),
            dma, dma, dma, dma, dma, dma, dma((6,)), dma((6,)), dma((8,)),
        ],
        compiler_params=pltpu.CompilerParams(
            vmem_limit_bytes=57 << 20, collective_id=0, has_side_effects=True),
    )(*ops)


def local(hidden, sw, filt, cot):
    mixed, gf, gs = run_kernel(hidden[0], cot[0], filt, jnp.swapaxes(sw, 0, 1))
    return mixed[None], gf, gs


def solution(mesh):
    in_specs = (P("dp", "ctx", None), P(), P(None, "ctx", None), P("dp", "ctx", None))
    out_specs = (P("dp", "ctx", None), P(None, "ctx", None), P(None, None, None, "ctx"))
    return jax.shard_map(local, mesh=mesh, in_specs=in_specs, out_specs=out_specs, check_vma=False)
```

```python
import functools

import numpy as np, ml_dtypes
import jax, jax.numpy as jnp
from jax import lax
from jax.experimental import pallas as pl
from jax.experimental.pallas import tpu as pltpu
from jax.sharding import PartitionSpec as P

BF = jnp.bfloat16
F32 = jnp.float32
NB = 64
LN = 128
CH = 16


def split(x):
    hi = x.astype(ml_dtypes.bfloat16)
    lo = (x - hi.astype(np.float64)).astype(ml_dtypes.bfloat16)
    return hi, lo


def constants():
    n = 2 * NB * LN
    k1 = np.arange(NB)[:, None] + 0.5
    n1 = np.arange(NB)[None, :]
    th = 2 * np.pi * k1 * n1 / LN
    a = np.concatenate([np.cos(th), -np.sin(th)], 0)
    b = np.concatenate([np.cos(th.T), -np.sin(th.T)], 1) * (2.0 / n)
    tw = 2 * np.pi * k1 * np.arange(LN)[None, :] / n
    twc, tws = np.cos(tw), np.sin(tw)
    ph = 2 * np.pi * np.outer(np.arange(LN), np.arange(LN)) / LN
    c, s = np.cos(ph), np.sin(ph)
    m = np.block([[c, -s], [s, c]])
    mi = np.block([[c, s], [-s, c]])
    ah, al = split(a)
    bh, bl = split(b)
    mh, ml = split(m)
    ih, il = split(mi)
    amat = np.concatenate([ah, ah, al], 1)
    bmat = np.concatenate([bh, bl], 1)
    tws = np.stack([twc, tws]).astype(np.float32)
    mats = np.stack([mh, ml, ih, il])
    return amat, bmat, tws, mats


def dot(a, b):
    return jnp.dot(a, b, preferred_element_type=F32)


def hilo(x):
    hi = x.astype(BF)
    return hi, (x - hi.astype(F32)).astype(BF)


def row_f(f):
    return f if f < 8 else 23 - f


def column(c, base=0, stride=CH):
    return pl.ds(base + c, NB, stride=stride)


def shift(x, k):
    m = x.shape[0] - 2
    lane = lax.broadcasted_iota(jnp.int32, (1, 1, LN), 2)
    if k == 0:
        return x[1:m + 1]
    if k > 0:
        r = pltpu.roll(x[0:m + 1], k, 2)
        return jnp.where(lane < k, r[0:m], r[1:m + 1])
    r = pltpu.roll(x[1:m + 2], LN + k, 2)
    return jnp.where(lane >= LN + k, r[1:m + 1], r[0:m])


def forward(src, base, spec, amat, tws, mats, zs, slot, chans, exact, precise):
    twc, tws_ = tws[0], tws[1]
    for pair in range(len(chans) // 2):
        x = jnp.concatenate([src[column(c, base), :] for c in chans[2 * pair:2 * pair + 2]], 1)
        hi, lo = hilo(x)
        if exact:
            p = dot(amat[:, 64:192], jnp.concatenate([hi, hi], 0))
        else:
            p = dot(amat[...], jnp.concatenate([hi, lo, hi], 0))
        for h in range(2):
            re = p[0:64, h * LN:(h + 1) * LN]
            im = p[64:128, h * LN:(h + 1) * LN]
            put(zs, slot + 2 * pair + h, re * twc + im * tws_, im * twc - re * tws_, precise)
    big(zs, slot * NB, spec, chans[0] * NB, len(chans) * NB, mats[0], mats[1], precise)


def big(zs, at, out, to, rows, mh, ml, precise):
    for r in range(0, rows, 256):
        zh = zs[0, at + r:at + r + 256, :]
        acc = dot(zh, mh)
        if precise > 0:
            acc = acc + dot(zh, ml)
        if precise > 1:
            acc = acc + dot(zs[1, at + r:at + r + 256, :], mh)
        out[to + r:to + r + 256, :] = acc


def put(zs, f, re, im, precise):
    z = jnp.concatenate([re, im], 1)
    zh, zl = hilo(z)
    zs[0, f * NB:(f + 1) * NB, :] = zh
    if precise > 1:
        zs[1, f * NB:(f + 1) * NB, :] = zl


def inverse(zs, slot, count, tmp, bmat, tws, mats, precise, store):
    big(zs, slot * NB, tmp, slot * NB, count * NB, mats[2], mats[3], precise)
    twc, tws_ = tws[0], tws[1]
    for pair in range(count // 2):
        us = []
        for h in range(2):
            r = (slot + 2 * pair + h) * NB
            re = tmp[r:r + NB, 0:LN]
            im = tmp[r:r + NB, LN:2 * LN]
            us.append(jnp.concatenate([re * twc - im * tws_, re * tws_ + im * twc], 0))
        u = jnp.concatenate(us, 1)
        uh, ul = hilo(u)
        y = dot(bmat[...], jnp.concatenate([uh, uh], 0))
        if precise > 1:
            y = y + dot(bmat[:, 0:128], ul)
        store(slot + 2 * pair, y[:, 0:LN])
        store(slot + 2 * pair + 1, y[:, LN:2 * LN])


def halves(ref, f):
    r = slice(f * NB, (f + 1) * NB)
    return ref[r, 0:LN], ref[r, LN:2 * LN]


def tap_rows(sw_ref, me, flipped, filter_order):
    row = lax.broadcasted_iota(jnp.int32, (CH, 1024), 0)
    lane = lax.broadcasted_iota(jnp.int32, (CH, 1024), 1)
    low = 8 * me + row
    if filter_order:
        high = 1023 - 8 * me - (row - 8)
    else:
        high = 1016 - 8 * me + (row - 8)
    chan = jnp.where(row < 8, low, high)
    if flipped:
        chan = 1023 - chan
    hit = lane == chan
    out = []
    for i in range(2):
        for k in range(3):
            w = sw_ref[k, i:i + 1, :]
            out.append(jnp.sum(jnp.where(hit, w, 0.0), axis=1, keepdims=True))
    return out


def wide(x):
    return jnp.broadcast_to(x, (CH, LN))[None]


STEP = 4
PIECES = 2
P_G, P_S, P_D, P_C, P_Q = 2, 1, 1, 1, 1
MESH = pl.DeviceIdType.MESH


def scatter(src, dst, send, recv):
    me = lax.axis_index("ctx")

    def one(o, _):
        q = lax.rem(me + o, NB)
        pltpu.make_async_remote_copy(
            src_ref=src.at[q], dst_ref=dst.at[me], send_sem=send, recv_sem=recv,
            device_id={"ctx": q}, device_id_type=MESH).start()
        return 0
    lax.fori_loop(1, NB, one, 0)
    dst[me] = src[me]


def await_all(ref, sem):
    part = ref.at[pl.ds(0, NB - 1)]
    pltpu.make_async_copy(part, part, sem).wait()


def to_chunks(get, dst):
    for j in range(4):
        low = get(j).T
        high = get(7 - j).T
        for g in range(16):
            both = jnp.concatenate([low[8 * g:8 * g + 8], high[120 - 8 * g:128 - 8 * g]], 0)
            dst[16 * j + g] = both.astype(BF)


def kernel(hid_h, cot_h, filt_h, sw_h, amat_h, bmat_h, tws_h, mats_h, mixed, gf, gs,
           hid, cot, filt, sw, amat, bmat, tws, mats,
           sendx, sendc, recvx, recvc, sendo, recvo,
           xrows, frows, qrows, conv_f, conv_r, gate_f, gate_r, buf, buf2,
           spec_s, spec_g, spec_d, tmp, tmp2, zs, zs2, half_out, half_in, pair_out, pair_in, small_in,
           sx, rx, sc, rc, so, ro, s2, r2, ins):
    pairs = ((hid_h, hid), (cot_h, cot), (filt_h, filt), (sw_h, sw), (amat_h, amat), (bmat_h, bmat), (tws_h, tws), (mats_h, mats))
    loads = [pltpu.make_async_copy(a, b, ins.at[i]) for i, (a, b) in enumerate(pairs)]
    for c in loads:
        c.start()
    me = lax.axis_index("ctx")
    dp = lax.axis_index("dp")
    core = lax.rem(dp, 2)
    yhi = dp // 2
    mate = yhi * 2 + 1 - core
    far = (1 - yhi) * 2 + core
    barrier = pltpu.get_barrier_semaphore()

    def greet(o, _):
        pl.semaphore_signal(barrier, inc=1, device_id={"ctx": lax.rem(me + o, NB)}, device_id_type=MESH)
        return 0
    lax.fori_loop(1, NB, greet, 0)
    for o in range(1, 4):
        pl.semaphore_signal(barrier, inc=1, device_id={"dp": lax.rem(dp + o, 4)}, device_id_type=MESH)

    every = list(range(CH))
    zero = jnp.zeros((CH, LN), F32)
    for p in (xrows, frows):
        p[0:CH] = zero
        p[(NB + 1) * CH:(NB + 2) * CH] = zero
    for h in range(2):
        qrows[h, 0:8] = zero[0:8]
        qrows[h, (NB + 1) * 8:(NB + 2) * 8] = zero[0:8]

    loads[0].wait()
    x = hid[...].astype(F32)
    scale = lax.rsqrt(jnp.mean(x * x, axis=1, keepdims=True) + 1e-06)
    to_chunks(lambda j: hid[:, j * LN:(j + 1) * LN].astype(F32) * scale, sendx)
    pl.semaphore_wait(barrier, NB - 1 + 3)
    scatter(sendx, recvx, sx, rx)
    loads[1].wait()
    to_chunks(lambda j: cot[:, j * LN:(j + 1) * LN].astype(F32), sendc)
    scatter(sendc, recvc, sc, rc)

    for c in loads[2:]:
        c.wait()
    wf = [wide(w) for w in tap_rows(sw, me, False, True)]
    wn = [wide(w) for w in tap_rows(sw, me, False, False)]
    wr = [wide(w) for w in tap_rows(sw, me, True, False)]

    for i in range(NB):
        frows[(i + 1) * CH:(i + 2) * CH] = filt[:, :, i * LN:(i + 1) * LN].astype(F32).reshape(CH, LN)

    def rows(i, more=0):
        return slice(i * STEP * CH, ((i + 1) * STEP + more) * CH)

    def tiles(ref, i, more=0):
        return ref[rows(i, more), :].reshape(STEP + more, CH, LN)

    for i in range(NB // STEP):
        v = tiles(frows, i, 2)
        g = wf[0] * shift(v, 0) + wf[1] * shift(v, 1) + wf[2] * shift(v, 2)
        buf[rows(i), :] = g.reshape(STEP * CH, LN)
    forward(buf, 0, spec_g, amat, tws, mats, zs, 0, every, False, P_G)

    await_all(recvx, rx)
    for i in range(NB):
        xrows[(i + 1) * CH:(i + 2) * CH] = recvx[i].astype(F32)
    forward(xrows, CH, spec_s, amat, tws, mats, zs, 0, every, True, P_S)

    for f in range(CH):
        r = row_f(f)
        gr, gi = halves(spec_g, f)
        sr, si = halves(spec_s, r)
        put(zs, r, gr * sr - gi * si, gr * si + gi * sr, P_C)
        sr, si = halves(spec_s, 15 - r)
        put(zs2, 15 - r, gr * sr + gi * si, gr * si - gi * sr, P_C)

    def keep(ref):
        def store(c, y):
            ref[column(c), :] = y
        return store
    inverse(zs, 0, CH, tmp, bmat, tws, mats, P_C, keep(conv_f))
    inverse(zs2, 0, CH, tmp2, bmat, tws, mats, P_C, keep(conv_r))
    for i in range(NB // STEP):
        v = tiles(xrows, i, 2)
        x0 = shift(v, 0)
        gf_ = wn[3] * x0 + wn[4] * shift(v, 1) + wn[5] * shift(v, 2)
        gr_ = wr[3] * x0 + wr[4] * shift(v, -1) + wr[5] * shift(v, -2)
        gate_f[rows(i), :] = gf_.reshape(STEP * CH, LN)
        gate_r[rows(i), :] = gr_.reshape(STEP * CH, LN)
        sendo[i * STEP:(i + 1) * STEP] = (gf_ * tiles(conv_f, i) + gr_ * tiles(conv_r, i)).astype(BF)
    scatter(sendo, recvo, so, ro)

    await_all(recvc, rc)
    for i in range(NB // STEP):
        ct = recvc[i * STEP:(i + 1) * STEP].astype(F32)
        buf[rows(i), :] = (ct * tiles(gate_f, i)).reshape(STEP * CH, LN)
        buf2[rows(i), :] = (ct * tiles(gate_r, i)).reshape(STEP * CH, LN)

    def q_half(h):
        own, other = every[8 * h:8 * h + 8], every[8 - 8 * h:16 - 8 * h]
        forward(buf, 0, spec_d, amat, tws, mats, zs, 0, own, False, P_D)
        forward(buf2, 0, spec_g, amat, tws, mats, zs, 8, other, False, P_D)
        for f in own:
            r = row_f(f)
            dr, di = halves(spec_d, r)
            sr, si = halves(spec_s, r)
            er, ei = halves(spec_g, 15 - r)
            tr, ti = halves(spec_s, 15 - r)
            put(zs2, f, dr * sr + di * si + er * tr + ei * ti, di * sr - dr * si + er * ti - ei * tr, P_Q)

        def store(f, y):
            qrows[h, column(f - 8 * h, 8, 8), :] = y
        inverse(zs2, 8 * h, 8, tmp, bmat, tws, mats, P_Q, store)
        for i in range(NB // STEP):
            v = qrows[h, i * STEP * 8:(i * STEP + STEP + 2) * 8, :].reshape(STEP + 2, 8, LN)
            g = 0.0
            for k in range(3):
                g = g + wf[k][:, 8 * h:8 * h + 8] * shift(v, -k)
            half_out[h, i * STEP:(i + 1) * STEP] = g

    for c in range(2):
        pl.when(core == c)(functools.partial(q_half, 1 - c))
    first = pltpu.make_async_remote_copy(
        src_ref=half_out.at[1 - core], dst_ref=half_in, send_sem=s2.at[0], recv_sem=r2.at[0],
        device_id={"dp": mate}, device_id_type=MESH)
    first.start()
    for c in range(2):
        pl.when(core == c)(functools.partial(q_half, c))
    first.wait()
    n = NB // 2 // PIECES
    seconds, thirds = [], []
    for p in range(PIECES):
        for i in range(p * n, (p + 1) * n):
            a = half_out[core, 2 * i:2 * i + 2] + half_in[2 * i:2 * i + 2]
            pair_out[i] = a.reshape(CH, LN).astype(BF)
        c = pltpu.make_async_remote_copy(
            src_ref=pair_out.at[pl.ds(p * n, n)], dst_ref=pair_in.at[pl.ds(p * n, n)],
            send_sem=s2.at[4 + p], recv_sem=r2.at[4 + p], device_id={"dp": far}, device_id_type=MESH)
        c.start()
        seconds.append(c)

    acc = [zero] * 9
    for i in range(NB // STEP):
        v = tiles(xrows, i, 2)
        ct = recvc[i * STEP:(i + 1) * STEP].astype(F32)
        cf = tiles(conv_f, i) * ct
        cr = tiles(conv_r, i) * ct
        fl = frows[(i * STEP + 1) * CH:((i + 1) * STEP + 1) * CH, :].reshape(STEP, CH, LN)
        q = jnp.concatenate([
            qrows[h, i * STEP * 8:(i * STEP + STEP + 2) * 8, :].reshape(STEP + 2, 8, LN) for h in range(2)], 1)
        for k in range(3):
            acc[k] = acc[k] + jnp.sum(fl * shift(q, -k), 0)
            acc[3 + k] = acc[3 + k] + jnp.sum(cf * shift(v, k), 0)
            acc[6 + k] = acc[6 + k] + jnp.sum(cr * shift(v, -k), 0)
    lane = lax.broadcasted_iota(jnp.int32, (CH, LN), 1)
    small = zero
    for k, a in enumerate(acc):
        small = jnp.where(lane == k, jnp.sum(a, 1, keepdims=True), small)
    small_in[dp] = small
    smalls = []
    for o in range(1, 4):
        c = pltpu.make_async_remote_copy(
            src_ref=small_in.at[dp], dst_ref=small_in.at[dp], send_sem=s2.at[o], recv_sem=r2.at[o],
            device_id={"dp": lax.rem(dp + o, 4)}, device_id_type=MESH)
        c.start()
        smalls.append(c)

    await_all(recvo, ro)
    for j in range(4):
        low = jnp.concatenate([recvo[16 * j + g].astype(F32)[0:8] for g in range(16)], 0)
        high = jnp.concatenate([recvo[16 * j + 15 - g].astype(F32)[8:16] for g in range(16)], 0)
        mixed[:, j * LN:(j + 1) * LN] = low.T.astype(BF)
        mixed[:, (7 - j) * LN:(8 - j) * LN] = high.T.astype(BF)

    for p in range(PIECES):
        seconds[p].wait()
        for i in range(p * n, (p + 1) * n):
            t = pair_out[i].astype(F32) + pair_in[i].astype(F32)
            gf[core, :, 2 * i * LN:(2 * i + 1) * LN] = t[0:8]
            gf[core, :, (2 * i + 1) * LN:(2 * i + 2) * LN] = t[8:16]
        part = gf.at[core, :, pl.ds(p * 2 * n * LN, 2 * n * LN)]
        c = pltpu.make_async_remote_copy(
            src_ref=part, dst_ref=part, send_sem=s2.at[4 + PIECES + p], recv_sem=r2.at[4 + PIECES + p],
            device_id={"dp": mate}, device_id_type=MESH)
        c.start()
        thirds.append(c)
    for c in smalls:
        c.wait()
    total = (small_in[0] + small_in[1]) + (small_in[2] + small_in[3])
    row = lax.broadcasted_iota(jnp.int32, (CH, LN), 0)

    def flat_rows(item, target):
        return jnp.sum(jnp.where(row == target, total[:, item:item + 1], 0.0), 0, keepdims=True)[:, 0:8]
    for k in range(3):
        gs[0, k] = jnp.concatenate([flat_rows(k, lane), flat_rows(k, lane + 8)], 0)
        gs[1, k] = jnp.concatenate([
            flat_rows(3 + k, lane) + flat_rows(6 + k, 15 - lane),
            flat_rows(3 + k, 15 - lane) + flat_rows(6 + k, lane)], 0)
    await_all(sendx, sx)
    await_all(sendc, sc)
    await_all(sendo, so)
    for c in thirds:
        c.wait()


def write(a, b, c, a_h, b_h, c_h, sems):
    copies = [pltpu.make_async_copy(x, y, sems.at[i]) for i, (x, y) in enumerate(((b, b_h), (a, a_h), (c, c_h)))]
    for x in copies:
        x.start()
    for x in copies:
        x.wait()


def run_kernel(hid, cot, filt, sw):
    amat, bmat, tws, mats = constants()
    vm = pl.BlockSpec(memory_space=pltpu.VMEM)
    dma = pltpu.SemaphoreType.DMA
    chunks = pltpu.VMEM((NB, CH, LN), BF)
    flat = pltpu.VMEM((NB * CH, LN), F32)
    padded = pltpu.VMEM(((NB + 2) * CH, LN), F32)
    spec = pltpu.VMEM((CH * NB, 2 * LN), F32)
    ops = (hid, cot, filt, sw, jnp.asarray(amat), jnp.asarray(bmat), jnp.asarray(tws), jnp.asarray(mats))
    held = [pltpu.VMEM(a.shape, a.dtype) for a in ops]
    outs = pl.pallas_call(
        kernel,
        out_shape=(
            pltpu.VMEM((LN, 1024), BF),
            pltpu.VMEM((2, 8, NB * LN), F32),
            pltpu.VMEM((2, 3, 2, 8), F32),
        ),
        in_specs=[pl.BlockSpec(memory_space=pltpu.HBM)] * 8,
        out_specs=(vm,) * 3,
        scratch_shapes=held + [chunks] * 6 + [padded] * 2 + [pltpu.VMEM((2, (NB + 2) * 8, LN), F32)] + [flat] * 6 + [spec] * 5 + [
            pltpu.VMEM((2, CH * NB, 2 * LN), BF),
            pltpu.VMEM((2, CH * NB, 2 * LN), BF),
            pltpu.VMEM((2, NB, 8, LN), F32),
            pltpu.VMEM((NB, 8, LN), F32),
            pltpu.VMEM((NB // 2, CH, LN), BF),
            pltpu.VMEM((NB // 2, CH, LN), BF),
            pltpu.VMEM((4, CH, LN), F32),
            dma, dma, dma, dma, dma, dma, dma((4 + 2 * PIECES,)), dma((4 + 2 * PIECES,)), dma((8,)),
        ],
        compiler_params=pltpu.CompilerParams(
            vmem_limit_bytes=57 << 20, collective_id=0, has_side_effects=True),
    )(*ops)
    return pl.pallas_call(
        write,
        out_shape=tuple(jax.ShapeDtypeStruct(a.shape, a.dtype) for a in outs),
        in_specs=[vm] * 3,
        out_specs=(pl.BlockSpec(memory_space=pltpu.HBM),) * 3,
        scratch_shapes=[dma((3,))],
        compiler_params=pltpu.CompilerParams(vmem_limit_bytes=1 << 20),
    )(*outs)


def local(hidden, sw, filt, cot):
    mixed, gf, gs = run_kernel(hidden[0], cot[0], filt, jnp.swapaxes(sw, 0, 1))
    return mixed[None], gf, gs


def solution(mesh):
    in_specs = (P("dp", "ctx", None), P(), P(None, "ctx", None), P("dp", "ctx", None))
    out_specs = (P("dp", "ctx", None), P(None, "ctx", None), P(None, None, None, "ctx"))
    return jax.shard_map(local, mesh=mesh, in_specs=in_specs, out_specs=out_specs, check_vma=False)
```

```python
import functools

import numpy as np, ml_dtypes
import jax, jax.numpy as jnp
from jax import lax
from jax.experimental import pallas as pl
from jax.experimental.pallas import tpu as pltpu
from jax.sharding import PartitionSpec as P

BF = jnp.bfloat16
F32 = jnp.float32
NB = 64
LN = 128
CH = 16
R = 8


def split(x):
    hi = x.astype(ml_dtypes.bfloat16)
    lo = (x - hi.astype(np.float64)).astype(ml_dtypes.bfloat16)
    return hi, lo


def constants():
    n = 2 * NB * LN
    k1 = np.arange(NB)[:, None] + 0.5
    n1 = np.arange(NB)[None, :]
    th = 2 * np.pi * k1 * n1 / LN
    a = np.concatenate([np.cos(th), -np.sin(th)], 0)
    b = np.concatenate([np.cos(th.T), -np.sin(th.T)], 1) * (2.0 / n)
    tw = 2 * np.pi * k1 * np.arange(LN)[None, :] / n
    twc, tws = np.cos(tw), np.sin(tw)
    ph = 2 * np.pi * np.outer(np.arange(LN), np.arange(LN)) / LN
    c, s = np.cos(ph), np.sin(ph)
    m = np.block([[c, -s], [s, c]])
    mi = np.block([[c, s], [-s, c]])
    ah, al = split(a)
    bh, bl = split(b)
    mh, ml = split(m)
    ih, il = split(mi)
    amat = np.concatenate([ah, ah, al], 1)
    bmat = np.concatenate([bh, bl], 1)
    tws = np.stack([twc, tws]).astype(np.float32)
    mats = np.stack([mh, ml, ih, il])
    return amat, bmat, tws, mats


def dot(a, b):
    return jnp.dot(a, b, preferred_element_type=F32)


def hilo(x):
    hi = x.astype(BF)
    return hi, (x - hi.astype(F32)).astype(BF)


ROW = ((0, 1, 2, 3, 7, 6, 5, 4), (3, 2, 1, 0, 4, 5, 6, 7))


def column(c, base=0):
    return pl.ds(base + c, NB, stride=R)


def shift(x, k):
    m = x.shape[0] - 2
    lane = lax.broadcasted_iota(jnp.int32, (1, 1, LN), 2)
    if k == 0:
        return x[1:m + 1]
    if k > 0:
        r = pltpu.roll(x[0:m + 1], k, 2)
        return jnp.where(lane < k, r[0:m], r[1:m + 1])
    r = pltpu.roll(x[1:m + 2], LN + k, 2)
    return jnp.where(lane >= LN + k, r[1:m + 1], r[0:m])


def forward(src, base, spec, to, amat, tws, mats, zs, exact, precise):
    twc, tws_ = tws[0], tws[1]
    for pair in range(R // 2):
        x = jnp.concatenate([src[column(c, base), :] for c in (2 * pair, 2 * pair + 1)], 1)
        hi, lo = hilo(x)
        if exact:
            p = dot(amat[:, 64:192], jnp.concatenate([hi, hi], 0))
        else:
            p = dot(amat[...], jnp.concatenate([hi, lo, hi], 0))
        for h in range(2):
            re = p[0:64, h * LN:(h + 1) * LN]
            im = p[64:128, h * LN:(h + 1) * LN]
            put(zs, to + 2 * pair + h, re * twc + im * tws_, im * twc - re * tws_, precise)
    big(zs, to * NB, spec, to * NB, R * NB, mats[0], mats[1], precise)


def big(zs, at, out, to, rows, mh, ml, precise):
    for r in range(0, rows, 256):
        zh = zs[0, at + r:at + r + 256, :]
        acc = dot(zh, mh)
        if precise > 0:
            acc = acc + dot(zh, ml)
        if precise > 1:
            acc = acc + dot(zs[1, at + r:at + r + 256, :], mh)
        out[to + r:to + r + 256, :] = acc


def put(zs, f, re, im, precise):
    z = jnp.concatenate([re, im], 1)
    zh, zl = hilo(z)
    zs[0, f * NB:(f + 1) * NB, :] = zh
    if precise > 1:
        zs[1, f * NB:(f + 1) * NB, :] = zl


def inverse(zs, slot, tmp, bmat, tws, mats, precise, store):
    big(zs, slot * NB, tmp, slot * NB, R * NB, mats[2], mats[3], precise)
    twc, tws_ = tws[0], tws[1]
    for pair in range(R // 2):
        us = []
        for h in range(2):
            r = (slot + 2 * pair + h) * NB
            re = tmp[r:r + NB, 0:LN]
            im = tmp[r:r + NB, LN:2 * LN]
            us.append(jnp.concatenate([re * twc - im * tws_, re * tws_ + im * twc], 0))
        u = jnp.concatenate(us, 1)
        uh, ul = hilo(u)
        y = dot(bmat[...], jnp.concatenate([uh, uh], 0))
        if precise > 1:
            y = y + dot(bmat[:, 0:128], ul)
        store(2 * pair, y[:, 0:LN])
        store(2 * pair + 1, y[:, LN:2 * LN])


def halves(ref, f):
    r = slice(f * NB, (f + 1) * NB)
    return ref[r, 0:LN], ref[r, LN:2 * LN]


def tap_rows(sw_ref, me, group, flipped, filter_order):
    row = lax.broadcasted_iota(jnp.int32, (R, 1024), 0)
    lane = lax.broadcasted_iota(jnp.int32, (R, 1024), 1)
    low = 8 * me + row
    high = 1016 - 8 * me + row
    if filter_order:
        high = 1016 - 8 * me + (11 - row if group == 0 else 3 - row)
    chan = jnp.where(row < 4, low, high) if group == 0 else jnp.where(row < 4, high, low)
    if flipped:
        chan = 1023 - chan
    hit = lane == chan
    out = []
    for i in range(2):
        for k in range(3):
            w = jnp.sum(jnp.where(hit, sw_ref[k, i:i + 1, :], 0.0), axis=1, keepdims=True)
            out.append(jnp.broadcast_to(w, (R, LN))[None])
    return out


STEP = 4
P_G, P_S, P_D, P_C, P_Q = 2, 1, 1, 1, 1
MESH = pl.DeviceIdType.MESH
HALF = NB // 2


def scatter(src, dst, send, recv):
    me = lax.axis_index("ctx")

    def one(o, _):
        q = lax.rem(me + o, NB)
        pltpu.make_async_remote_copy(
            src_ref=src.at[q], dst_ref=dst.at[me], send_sem=send, recv_sem=recv,
            device_id={"ctx": q}, device_id_type=MESH).start()
        return 0
    lax.fori_loop(1, NB, one, 0)
    dst[me] = src[me]


def await_all(ref, sem):
    part = ref.at[pl.ds(0, NB - 1)]
    pltpu.make_async_copy(part, part, sem).wait()


def kernel(hid_h, cot_h, filt_h, sw_h, amat_h, bmat_h, tws_h, mats_h, mixed, gf, gs,
           hid, cot, filt, sw, amat, bmat, tws, mats,
           sends, recvs, sendo, recvo,
           xrows, crows, frows, qrows, conv_f, conv_r, gate_f, gate_r, mixes, buf, buf2,
           spec_s, spec_g, spec_d, spec_e, tmp, tmp2, zs, zs2, half_out, half_in, pair_out, pair_in, small_in,
           ss, rs, so, ro, s2, r2, ins):
    pairs = ((hid_h, hid), (cot_h, cot), (filt_h, filt), (sw_h, sw), (amat_h, amat), (bmat_h, bmat), (tws_h, tws), (mats_h, mats))
    loads = [pltpu.make_async_copy(a, b, ins.at[i]) for i, (a, b) in enumerate(pairs)]
    for c in loads:
        c.start()
    me = lax.axis_index("ctx")
    dp = lax.axis_index("dp")
    core = lax.rem(dp, 2)
    yhi = dp // 2
    mate = yhi * 2 + 1 - core
    far = (1 - yhi) * 2 + core
    barrier = pltpu.get_barrier_semaphore()

    def greet(o, _):
        pl.semaphore_signal(barrier, inc=1, device_id={"ctx": lax.rem(me + o, NB)}, device_id_type=MESH)
        return 0
    lax.fori_loop(1, NB, greet, 0)
    for o in range(1, 4):
        pl.semaphore_signal(barrier, inc=1, device_id={"dp": lax.rem(dp + o, 4)}, device_id_type=MESH)

    zero = jnp.zeros((R, LN), F32)
    upper = lax.broadcasted_iota(jnp.int32, (R, LN), 0) < 4
    for g in range(2):
        for p in (xrows, frows, qrows):
            p[g, 0:R] = zero
            p[g, (NB + 1) * R:(NB + 2) * R] = zero

    loads[0].wait()
    x = hid[...].astype(F32)
    scale = lax.rsqrt(jnp.mean(x * x, axis=1, keepdims=True) + 1e-06)
    loads[1].wait()

    def block(j):
        at = slice(j * LN, (j + 1) * LN)
        return (hid[:, at].astype(F32) * scale).T, cot[:, at].astype(F32).T
    for j in range(4):
        low, high = block(j), block(7 - j)
        for i in range(16):
            a = [v[8 * i:8 * i + 8] for v in low]
            b = [v[120 - 8 * i:128 - 8 * i] for v in high]
            sends[0, 16 * j + i] = jnp.concatenate([jnp.where(upper, u, v) for u, v in zip(a, b)], 0).astype(BF)
            sends[1, 16 * j + i] = jnp.concatenate([jnp.where(upper, v, u) for u, v in zip(a, b)], 0).astype(BF)
    pl.semaphore_wait(barrier, NB - 1 + 3)
    for g in range(2):
        scatter(sends.at[g], recvs.at[g], ss.at[g], rs.at[g])

    for c in loads[2:]:
        c.wait()
    wf = [tap_rows(sw, me, g, False, True) for g in range(2)]
    wn = [tap_rows(sw, me, g, False, False) for g in range(2)]
    wr = [tap_rows(sw, me, g, True, False) for g in range(2)]

    def rows(i, more=0):
        return slice(i * STEP * R, ((i + 1) * STEP + more) * R)

    def tiles(ref, g, i, more=0):
        return ref[g, rows(i, more), :].reshape(STEP + more, R, LN)

    def flat(v):
        return v.reshape(STEP * R, LN)

    for i in range(NB):
        a = filt[0, :, i * LN:(i + 1) * LN].astype(F32)
        b = pltpu.roll(filt[1, :, i * LN:(i + 1) * LN].astype(F32), 4, 0)
        frows[0, (i + 1) * R:(i + 2) * R] = jnp.where(upper, a, b)
        frows[1, (i + 1) * R:(i + 2) * R] = jnp.where(upper, b, a)
    for g in range(2):
        for i in range(NB // STEP):
            v = tiles(frows, g, i, 2)
            buf[g, rows(i), :] = flat(wf[g][0] * shift(v, 0) + wf[g][1] * shift(v, 1) + wf[g][2] * shift(v, 2))
        forward(buf.at[g], 0, spec_g, g * R, amat, tws, mats, zs, False, P_G)

    def keep(ref, g, base=0):
        def store(c, y):
            ref[g, column(c, base), :] = y
        return store

    def outputs(g):
        await_all(recvs.at[g], rs.at[g])
        for i in range(NB):
            v = recvs[g, i].astype(F32)
            xrows[g, (i + 1) * R:(i + 2) * R] = v[0:R]
            crows[g, i * R:(i + 1) * R] = v[R:2 * R]
        forward(xrows.at[g], R, spec_s, g * R, amat, tws, mats, zs, True, P_S)
        for f in range(R):
            r = ROW[g][f]
            gr, gi = halves(spec_g, g * R + f)
            sr, si = halves(spec_s, g * R + r)
            put(zs, g * R + r, gr * sr - gi * si, gr * si + gi * sr, P_C)
            sr, si = halves(spec_s, g * R + 7 - r)
            put(zs2, g * R + 7 - r, gr * sr + gi * si, gr * si - gi * sr, P_C)
        inverse(zs, g * R, tmp, bmat, tws, mats, P_C, keep(conv_f, g))
        inverse(zs2, g * R, tmp2, bmat, tws, mats, P_C, keep(conv_r, g))
        n, r = wn[g], wr[g]
        for i in range(NB // STEP):
            v = tiles(xrows, g, i, 2)
            x0 = shift(v, 0)
            a = n[3] * x0 + n[4] * shift(v, 1) + n[5] * shift(v, 2)
            b = r[3] * x0 + r[4] * shift(v, -1) + r[5] * shift(v, -2)
            gate_f[g, rows(i), :] = flat(a)
            gate_r[g, rows(i), :] = flat(b)
            m = a * tiles(conv_f, g, i) + b * tiles(conv_r, g, i)
            if g == 0:
                mixes[0, rows(i), :] = flat(m)
            else:
                sendo[i * STEP:(i + 1) * STEP] = jnp.concatenate([tiles(mixes, 0, i), m], 1).astype(BF)

    def gradients(g):
        for i in range(NB // STEP):
            ct = tiles(crows, g, i)
            buf[g, rows(i), :] = flat(ct * tiles(gate_f, g, i))
            buf2[g, rows(i), :] = flat(ct * tiles(gate_r, g, i))
        forward(buf.at[g], 0, spec_d, g * R, amat, tws, mats, zs, False, P_D)
        forward(buf2.at[g], 0, spec_e, g * R, amat, tws, mats, zs2, False, P_D)
        for f in range(R):
            r = ROW[g][f]
            dr, di = halves(spec_d, g * R + r)
            sr, si = halves(spec_s, g * R + r)
            er, ei = halves(spec_e, g * R + 7 - r)
            tr, ti = halves(spec_s, g * R + 7 - r)
            put(zs, g * R + f, dr * sr + di * si + er * tr + ei * ti, di * sr - dr * si + er * ti - ei * tr, P_Q)
        inverse(zs, g * R, tmp, bmat, tws, mats, P_Q, keep(qrows, g, R))
        for i in range(NB // STEP):
            v = tiles(qrows, g, i, 2)
            half_out[g, i * STEP:(i + 1) * STEP] = sum(wf[g][k] * shift(v, -k) for k in range(3))
        c = pltpu.make_async_remote_copy(
            src_ref=half_out.at[g, pl.ds((1 - core) * HALF, HALF)], dst_ref=half_in.at[g],
            send_sem=s2.at[4 + g], recv_sem=r2.at[4 + g], device_id={"dp": mate}, device_id_type=MESH)
        c.start()
        return c

    def between_chips(g, first):
        first.wait()
        for i in range(HALF // 2):
            a = half_out[g, pl.ds(core * HALF + 2 * i, 2)] + half_in[g, 2 * i:2 * i + 2]
            pair_out[g, i] = a.reshape(CH, LN).astype(BF)
        c = pltpu.make_async_remote_copy(
            src_ref=pair_out.at[g], dst_ref=pair_in.at[g], send_sem=s2.at[6 + g], recv_sem=r2.at[6 + g],
            device_id={"dp": far}, device_id_type=MESH)
        c.start()
        return c

    def tap_sums(g):
        acc = [zero] * 9
        for i in range(NB // STEP):
            v = tiles(xrows, g, i, 2)
            ct = tiles(crows, g, i)
            cf = tiles(conv_f, g, i) * ct
            cr = tiles(conv_r, g, i) * ct
            fl = frows[g, (i * STEP + 1) * R:((i + 1) * STEP + 1) * R, :].reshape(STEP, R, LN)
            q = tiles(qrows, g, i, 2)
            for k in range(3):
                acc[k] = acc[k] + jnp.sum(fl * shift(q, -k), 0)
                acc[3 + k] = acc[3 + k] + jnp.sum(cf * shift(v, k), 0)
                acc[6 + k] = acc[6 + k] + jnp.sum(cr * shift(v, -k), 0)
        lane = lax.broadcasted_iota(jnp.int32, (R, LN), 1)
        small = zero
        for k, a in enumerate(acc):
            small = jnp.where(lane == k, jnp.sum(a, 1, keepdims=True), small)
        return small

    outputs(0)
    first0 = gradients(0)
    second0 = between_chips(0, first0)
    outputs(1)
    scatter(sendo, recvo, so, ro)
    first1 = gradients(1)
    small0 = tap_sums(0)
    second1 = between_chips(1, first1)
    small_in[dp] = jnp.concatenate([small0, tap_sums(1)], 0)
    smalls = []
    for o in range(1, 4):
        c = pltpu.make_async_remote_copy(
            src_ref=small_in.at[dp], dst_ref=small_in.at[dp], send_sem=s2.at[o], recv_sem=r2.at[o],
            device_id={"dp": lax.rem(dp + o, 4)}, device_id_type=MESH)
        c.start()
        smalls.append(c)

    await_all(recvo, ro)
    for j in range(4):
        low, high = [], []
        for i in range(16):
            v = recvo[16 * j + i].astype(F32)
            low.append(jnp.where(upper, v[0:R], v[R:2 * R]))
            high.append(jnp.where(upper, v[R:2 * R], v[0:R]))
        mixed[:, j * LN:(j + 1) * LN] = jnp.concatenate(low, 0).T.astype(BF)
        mixed[:, (7 - j) * LN:(8 - j) * LN] = jnp.concatenate(high[::-1], 0).T.astype(BF)

    second0.wait()
    second1.wait()
    for i in range(HALF // 2):
        a, b = [pair_out[g, i].astype(F32) + pair_in[g, i].astype(F32) for g in range(2)]
        for h in range(2):
            at = pl.ds(pl.multiple_of((core * HALF + 2 * i + h) * LN, LN), LN)
            u, v = a[R * h:R * h + R], b[R * h:R * h + R]
            gf[0, :, at] = jnp.where(upper, u, v)
            gf[1, :, at] = pltpu.roll(jnp.where(upper, v, u), 4, 0)
    part = gf.at[:, :, pl.ds(pl.multiple_of(core * HALF * LN, HALF * LN), HALF * LN)]
    third = pltpu.make_async_remote_copy(
        src_ref=part, dst_ref=part, send_sem=s2.at[0], recv_sem=r2.at[0],
        device_id={"dp": mate}, device_id_type=MESH)
    third.start()
    for c in smalls:
        c.wait()
    total = (small_in[0] + small_in[1]) + (small_in[2] + small_in[3])
    row = lax.broadcasted_iota(jnp.int32, (CH, LN), 0)
    lane = lax.broadcasted_iota(jnp.int32, (CH, LN), 1)
    near = jnp.where(lane < 4, lane, lane + 8)
    other = jnp.where(lane < 4, 7 - lane, 15 - lane)

    def pick(item, target):
        return jnp.sum(jnp.where(row == target, total[:, item:item + 1], 0.0), 0, keepdims=True)[:, 0:8]
    for k in range(3):
        gs[0, k] = jnp.concatenate([pick(k, near), pick(k, lane + 4)], 0)
        gs[1, k] = jnp.concatenate([pick(3 + k, near) + pick(6 + k, other), pick(3 + k, other) + pick(6 + k, near)], 0)
    for g in range(2):
        await_all(sends.at[g], ss.at[g])
    await_all(sendo, so)
    third.wait()


def write(a, b, c, a_h, b_h, c_h, sems):
    copies = [pltpu.make_async_copy(x, y, sems.at[i]) for i, (x, y) in enumerate(((b, b_h), (a, a_h), (c, c_h)))]
    for x in copies:
        x.start()
    for x in copies:
        x.wait()


def run_kernel(hid, cot, filt, sw):
    amat, bmat, tws, mats = constants()
    vm = pl.BlockSpec(memory_space=pltpu.VMEM)
    dma = pltpu.SemaphoreType.DMA
    def group(blocks, dtype=F32):
        return pltpu.VMEM((2, blocks * R, LN), dtype)
    chunks = pltpu.VMEM((NB, CH, LN), BF)
    both = pltpu.VMEM((2, NB, CH, LN), BF)
    spec = pltpu.VMEM((CH * NB, 2 * LN), F32)
    split_spec = pltpu.VMEM((2, CH * NB, 2 * LN), BF)
    ops = (hid, cot, filt, sw, jnp.asarray(amat), jnp.asarray(bmat), jnp.asarray(tws), jnp.asarray(mats))
    held = [pltpu.VMEM(a.shape, a.dtype) for a in ops]
    outs = pl.pallas_call(
        kernel,
        out_shape=(
            pltpu.VMEM((LN, 1024), BF),
            pltpu.VMEM((2, 8, NB * LN), F32),
            pltpu.VMEM((2, 3, 2, 8), F32),
        ),
        in_specs=[pl.BlockSpec(memory_space=pltpu.HBM)] * 8,
        out_specs=(vm,) * 3,
        scratch_shapes=held + [both] * 2 + [chunks] * 2 + [
            group(NB + 2), group(NB), group(NB + 2), group(NB + 2)] + [group(NB)] * 7 + [spec] * 6 + [split_spec] * 2 + [
            pltpu.VMEM((2, NB, R, LN), F32),
            pltpu.VMEM((2, HALF, R, LN), F32),
            pltpu.VMEM((2, HALF // 2, CH, LN), BF),
            pltpu.VMEM((2, HALF // 2, CH, LN), BF),
            pltpu.VMEM((4, CH, LN), F32),
            dma((2,)), dma((2,)), dma, dma, dma((8,)), dma((8,)), dma((8,)),
        ],
        compiler_params=pltpu.CompilerParams(
            vmem_limit_bytes=57 << 20, collective_id=0, has_side_effects=True),
    )(*ops)
    return pl.pallas_call(
        write,
        out_shape=tuple(jax.ShapeDtypeStruct(a.shape, a.dtype) for a in outs),
        in_specs=[vm] * 3,
        out_specs=(pl.BlockSpec(memory_space=pltpu.HBM),) * 3,
        scratch_shapes=[dma((3,))],
        compiler_params=pltpu.CompilerParams(vmem_limit_bytes=1 << 20),
    )(*outs)


def local(hidden, sw, filt, cot):
    mixed, gf, gs = run_kernel(hidden[0], cot[0], filt, jnp.swapaxes(sw, 0, 1))
    return mixed[None], gf, gs


def solution(mesh):
    in_specs = (P("dp", "ctx", None), P(), P(None, "ctx", None), P("dp", "ctx", None))
    out_specs = (P("dp", "ctx", None), P(None, "ctx", None), P(None, None, None, "ctx"))
    return jax.shard_map(local, mesh=mesh, in_specs=in_specs, out_specs=out_specs, check_vma=False)
```

```python
import functools

import numpy as np, ml_dtypes
import jax, jax.numpy as jnp
from jax import lax
from jax.experimental import pallas as pl
from jax.experimental.pallas import tpu as pltpu
from jax.sharding import PartitionSpec as P

BF = jnp.bfloat16
F32 = jnp.float32
NB = 64
LN = 128
CH = 16


def split(x):
    hi = x.astype(ml_dtypes.bfloat16)
    lo = (x - hi.astype(np.float64)).astype(ml_dtypes.bfloat16)
    return hi, lo


def constants():
    n = 2 * NB * LN
    k1 = np.arange(NB)[:, None] + 0.5
    n1 = np.arange(NB)[None, :]
    th = 2 * np.pi * k1 * n1 / LN
    a = np.concatenate([np.cos(th), -np.sin(th)], 0)
    b = np.concatenate([np.cos(th.T), -np.sin(th.T)], 1) * (2.0 / n)
    tw = 2 * np.pi * k1 * np.arange(LN)[None, :] / n
    twc, tws = np.cos(tw), np.sin(tw)
    ph = 2 * np.pi * np.outer(np.arange(LN), np.arange(LN)) / LN
    c, s = np.cos(ph), np.sin(ph)
    m = np.block([[c, -s], [s, c]])
    mi = np.block([[c, s], [-s, c]])
    ah, al = split(a)
    bh, bl = split(b)
    mh, ml = split(m)
    ih, il = split(mi)
    amat = np.concatenate([ah, ah, al], 1)
    bmat = np.concatenate([bh, bl], 1)
    tws = np.stack([twc, tws]).astype(np.float32)
    mats = np.stack([mh, ml, ih, il])
    return amat, bmat, tws, mats


def dot(a, b):
    return jnp.dot(a, b, preferred_element_type=F32)


def hilo(x):
    hi = x.astype(BF)
    return hi, (x - hi.astype(F32)).astype(BF)


def row_f(f):
    return f if f < 8 else 23 - f


def column(c, base=0, stride=CH):
    return pl.ds(base + c, NB, stride=stride)


def shift(x, k):
    m = x.shape[0] - 2
    lane = lax.broadcasted_iota(jnp.int32, (1, 1, LN), 2)
    if k == 0:
        return x[1:m + 1]
    if k > 0:
        r = pltpu.roll(x[0:m + 1], k, 2)
        return jnp.where(lane < k, r[0:m], r[1:m + 1])
    r = pltpu.roll(x[1:m + 2], LN + k, 2)
    return jnp.where(lane >= LN + k, r[1:m + 1], r[0:m])


def forward(src, base, spec, amat, tws, mats, zs, slot, chans, exact, precise):
    twc, tws_ = tws[0], tws[1]
    for pair in range(len(chans) // 2):
        x = jnp.concatenate([src[column(c, base), :] for c in chans[2 * pair:2 * pair + 2]], 1)
        hi, lo = hilo(x)
        if exact:
            p = dot(amat[:, 64:192], jnp.concatenate([hi, hi], 0))
        else:
            p = dot(amat[...], jnp.concatenate([hi, lo, hi], 0))
        for h in range(2):
            re = p[0:64, h * LN:(h + 1) * LN]
            im = p[64:128, h * LN:(h + 1) * LN]
            put(zs, slot + 2 * pair + h, re * twc + im * tws_, im * twc - re * tws_, precise)
    big(zs, slot * NB, spec, chans[0] * NB, len(chans) * NB, mats[0], mats[1], precise)


def big(zs, at, out, to, rows, mh, ml, precise):
    for r in range(0, rows, 256):
        zh = zs[0, at + r:at + r + 256, :]
        acc = dot(zh, mh)
        if precise > 0:
            acc = acc + dot(zh, ml)
        if precise > 1:
            acc = acc + dot(zs[1, at + r:at + r + 256, :], mh)
        out[to + r:to + r + 256, :] = acc


def put(zs, f, re, im, precise):
    z = jnp.concatenate([re, im], 1)
    zh, zl = hilo(z)
    zs[0, f * NB:(f + 1) * NB, :] = zh
    if precise > 1:
        zs[1, f * NB:(f + 1) * NB, :] = zl


def inverse(zs, slot, count, tmp, bmat, tws, mats, precise, store):
    big(zs, slot * NB, tmp, slot * NB, count * NB, mats[2], mats[3], precise)
    twc, tws_ = tws[0], tws[1]
    for pair in range(count // 2):
        us = []
        for h in range(2):
            r = (slot + 2 * pair + h) * NB
            re = tmp[r:r + NB, 0:LN]
            im = tmp[r:r + NB, LN:2 * LN]
            us.append(jnp.concatenate([re * twc - im * tws_, re * tws_ + im * twc], 0))
        u = jnp.concatenate(us, 1)
        uh, ul = hilo(u)
        y = dot(bmat[...], jnp.concatenate([uh, uh], 0))
        if precise > 1:
            y = y + dot(bmat[:, 0:128], ul)
        store(slot + 2 * pair, y[:, 0:LN])
        store(slot + 2 * pair + 1, y[:, LN:2 * LN])


def halves(ref, f):
    r = slice(f * NB, (f + 1) * NB)
    return ref[r, 0:LN], ref[r, LN:2 * LN]


def tap_rows(sw_ref, me, flipped, filter_order):
    row = lax.broadcasted_iota(jnp.int32, (CH, 1024), 0)
    lane = lax.broadcasted_iota(jnp.int32, (CH, 1024), 1)
    low = 8 * me + row
    if filter_order:
        high = 1023 - 8 * me - (row - 8)
    else:
        high = 1016 - 8 * me + (row - 8)
    chan = jnp.where(row < 8, low, high)
    if flipped:
        chan = 1023 - chan
    hit = lane == chan
    out = []
    for i in range(2):
        for k in range(3):
            w = sw_ref[k, i:i + 1, :]
            out.append(jnp.sum(jnp.where(hit, w, 0.0), axis=1, keepdims=True))
    return out


def wide(x):
    return jnp.broadcast_to(x, (CH, LN))[None]


STEP = 4
PIECES = 4
P_G, P_S, P_D, P_C, P_Q = 2, 1, 1, 1, 1
MESH = pl.DeviceIdType.MESH


def scatter(src, dst, send, recv):
    me = lax.axis_index("ctx")

    def one(o, _):
        q = lax.rem(me + o, NB)
        pltpu.make_async_remote_copy(
            src_ref=src.at[q], dst_ref=dst.at[me], send_sem=send, recv_sem=recv,
            device_id={"ctx": q}, device_id_type=MESH).start()
        return 0
    lax.fori_loop(1, NB, one, 0, unroll=9)
    dst[me] = src[me]


def await_all(ref, sem):
    part = ref.at[pl.ds(0, NB - 1)]
    pltpu.make_async_copy(part, part, sem).wait()


def to_chunks(get, dst):
    for j in range(4):
        low = get(j).T
        high = get(7 - j).T
        for g in range(16):
            both = jnp.concatenate([low[8 * g:8 * g + 8], high[120 - 8 * g:128 - 8 * g]], 0)
            dst[16 * j + g] = both.astype(BF)


def kernel(hid_h, cot_h, filt_h, sw_h, amat_h, bmat_h, tws_h, mats_h, mixed, gf, gs,
           hid, cot, filt, sw, amat, bmat, tws, mats,
           sendx, sendc, recvx, recvc, sendo, recvo,
           xrows, frows, qrows, conv_f, conv_r, gate_f, gate_r, buf, buf2,
           spec_s, spec_g, spec_d, tmp, tmp2, zs, zs2, half_out, half_send, half_in, pair_out, pair_in, small_in,
           sx, rx, sc, rc, so, ro, s2, r2, ins):
    pairs = ((hid_h, hid), (cot_h, cot), (filt_h, filt), (sw_h, sw), (amat_h, amat), (bmat_h, bmat), (tws_h, tws), (mats_h, mats))
    loads = [pltpu.make_async_copy(a, b, ins.at[i]) for i, (a, b) in enumerate(pairs)]
    for c in loads:
        c.start()
    me = lax.axis_index("ctx")
    dp = lax.axis_index("dp")
    core = lax.rem(dp, 2)
    yhi = dp // 2
    mate = yhi * 2 + 1 - core
    far = (1 - yhi) * 2 + core
    barrier = pltpu.get_barrier_semaphore()

    def greet(o, _):
        pl.semaphore_signal(barrier, inc=1, device_id={"ctx": lax.rem(me + o, NB)}, device_id_type=MESH)
        return 0
    lax.fori_loop(1, NB, greet, 0, unroll=9)
    for o in range(1, 4):
        pl.semaphore_signal(barrier, inc=1, device_id={"dp": lax.rem(dp + o, 4)}, device_id_type=MESH)

    every = list(range(CH))
    zero = jnp.zeros((CH, LN), F32)
    for p in (xrows, frows):
        p[0:CH] = zero
        p[(NB + 1) * CH:(NB + 2) * CH] = zero
    for h in range(2):
        qrows[h, 0:8] = zero[0:8]
        qrows[h, (NB + 1) * 8:(NB + 2) * 8] = zero[0:8]

    loads[0].wait()
    x = hid[...].astype(F32)
    scale = lax.rsqrt(jnp.mean(x * x, axis=1, keepdims=True) + 1e-06)
    to_chunks(lambda j: hid[:, j * LN:(j + 1) * LN].astype(F32) * scale, sendx)
    pl.semaphore_wait(barrier, NB - 1 + 3)
    scatter(sendx, recvx, sx, rx)
    loads[1].wait()
    to_chunks(lambda j: cot[:, j * LN:(j + 1) * LN].astype(F32), sendc)
    scatter(sendc, recvc, sc, rc)

    for c in loads[2:]:
        c.wait()
    wf = [wide(w) for w in tap_rows(sw, me, False, True)]
    wn = [wide(w) for w in tap_rows(sw, me, False, False)]
    wr = [wide(w) for w in tap_rows(sw, me, True, False)]

    for i in range(NB):
        frows[(i + 1) * CH:(i + 2) * CH] = filt[:, :, i * LN:(i + 1) * LN].astype(F32).reshape(CH, LN)

    def rows(i, more=0):
        return slice(i * STEP * CH, ((i + 1) * STEP + more) * CH)

    def tiles(ref, i, more=0):
        return ref[rows(i, more), :].reshape(STEP + more, CH, LN)

    for i in range(NB // STEP):
        v = tiles(frows, i, 2)
        g = wf[0] * shift(v, 0) + wf[1] * shift(v, 1) + wf[2] * shift(v, 2)
        buf[rows(i), :] = g.reshape(STEP * CH, LN)
    forward(buf, 0, spec_g, amat, tws, mats, zs, 0, every, False, P_G)

    await_all(recvx, rx)
    for i in range(NB):
        xrows[(i + 1) * CH:(i + 2) * CH] = recvx[i].astype(F32)
    forward(xrows, CH, spec_s, amat, tws, mats, zs, 0, every, True, P_S)

    for f in range(CH):
        r = row_f(f)
        gr, gi = halves(spec_g, f)
        sr, si = halves(spec_s, r)
        put(zs, r, gr * sr - gi * si, gr * si + gi * sr, P_C)
        sr, si = halves(spec_s, 15 - r)
        put(zs2, 15 - r, gr * sr + gi * si, gr * si - gi * sr, P_C)

    def keep(ref):
        def store(c, y):
            ref[column(c), :] = y
        return store
    inverse(zs, 0, CH, tmp, bmat, tws, mats, P_C, keep(conv_f))
    inverse(zs2, 0, CH, tmp2, bmat, tws, mats, P_C, keep(conv_r))
    for i in range(NB // STEP):
        v = tiles(xrows, i, 2)
        x0 = shift(v, 0)
        gf_ = wn[3] * x0 + wn[4] * shift(v, 1) + wn[5] * shift(v, 2)
        gr_ = wr[3] * x0 + wr[4] * shift(v, -1) + wr[5] * shift(v, -2)
        gate_f[rows(i), :] = gf_.reshape(STEP * CH, LN)
        gate_r[rows(i), :] = gr_.reshape(STEP * CH, LN)
        sendo[i * STEP:(i + 1) * STEP] = (gf_ * tiles(conv_f, i) + gr_ * tiles(conv_r, i)).astype(BF)
    scatter(sendo, recvo, so, ro)

    await_all(recvc, rc)
    def q_half(h, mine):
        own, other = every[8 * h:8 * h + 8], every[8 - 8 * h:16 - 8 * h]
        for i in range(NB):
            ct = recvc[i].astype(F32)
            u = slice(i * CH + 8 * h, i * CH + 8 * h + 8)
            v = slice(i * CH + 8 - 8 * h, i * CH + 16 - 8 * h)
            buf[u, :] = ct[8 * h:8 * h + 8] * gate_f[u, :]
            buf2[v, :] = ct[8 - 8 * h:16 - 8 * h] * gate_r[v, :]
        forward(buf, 0, spec_d, amat, tws, mats, zs, 0, own, False, P_D)
        forward(buf2, 0, spec_g, amat, tws, mats, zs, 8, other, False, P_D)
        for f in own:
            r = row_f(f)
            dr, di = halves(spec_d, r)
            sr, si = halves(spec_s, r)
            er, ei = halves(spec_g, 15 - r)
            tr, ti = halves(spec_s, 15 - r)
            put(zs2, f, dr * sr + di * si + er * tr + ei * ti, di * sr - dr * si + er * ti - ei * tr, P_Q)

        def store(f, y):
            qrows[h, column(f - 8 * h, 8, 8), :] = y
        inverse(zs2, 8 * h, 8, tmp, bmat, tws, mats, P_Q, store)
        for i in range(NB // STEP):
            v = qrows[h, i * STEP * 8:(i * STEP + STEP + 2) * 8, :].reshape(STEP + 2, 8, LN)
            g = 0.0
            for k in range(3):
                g = g + wf[k][:, 8 * h:8 * h + 8] * shift(v, -k)
            g = g.reshape(STEP // 2, CH, LN)
            if mine:
                half_out[i * STEP // 2:(i + 1) * STEP // 2] = g
            else:
                half_send[i * STEP // 2:(i + 1) * STEP // 2] = g.astype(BF)

    for c in range(2):
        pl.when(core == c)(functools.partial(q_half, 1 - c, False))
    first = pltpu.make_async_remote_copy(
        src_ref=half_send, dst_ref=half_in, send_sem=s2.at[0], recv_sem=r2.at[0],
        device_id={"dp": mate}, device_id_type=MESH)
    first.start()
    for c in range(2):
        pl.when(core == c)(functools.partial(q_half, c, True))
    first.wait()
    n = NB // 2 // PIECES
    seconds, thirds = [], []
    for p in range(PIECES):
        for i in range(p * n, (p + 1) * n):
            pair_out[i] = (half_out[i] + half_in[i].astype(F32)).astype(BF)
        c = pltpu.make_async_remote_copy(
            src_ref=pair_out.at[pl.ds(p * n, n)], dst_ref=pair_in.at[pl.ds(p * n, n)],
            send_sem=s2.at[4 + p], recv_sem=r2.at[4 + p], device_id={"dp": far}, device_id_type=MESH)
        c.start()
        seconds.append(c)

    acc = [zero] * 9
    for i in range(NB // STEP):
        v = tiles(xrows, i, 2)
        ct = recvc[i * STEP:(i + 1) * STEP].astype(F32)
        cf = tiles(conv_f, i) * ct
        cr = tiles(conv_r, i) * ct
        fl = frows[(i * STEP + 1) * CH:((i + 1) * STEP + 1) * CH, :].reshape(STEP, CH, LN)
        q = jnp.concatenate([
            qrows[h, i * STEP * 8:(i * STEP + STEP + 2) * 8, :].reshape(STEP + 2, 8, LN) for h in range(2)], 1)
        for k in range(3):
            acc[k] = acc[k] + jnp.sum(fl * shift(q, -k), 0)
            acc[3 + k] = acc[3 + k] + jnp.sum(cf * shift(v, k), 0)
            acc[6 + k] = acc[6 + k] + jnp.sum(cr * shift(v, -k), 0)
    lane = lax.broadcasted_iota(jnp.int32, (CH, LN), 1)
    small = zero
    for k, a in enumerate(acc):
        small = jnp.where(lane == k, jnp.sum(a, 1, keepdims=True), small)
    small_in[dp] = small
    smalls = []
    for o in range(1, 4):
        c = pltpu.make_async_remote_copy(
            src_ref=small_in.at[dp], dst_ref=small_in.at[dp], send_sem=s2.at[o], recv_sem=r2.at[o],
            device_id={"dp": lax.rem(dp + o, 4)}, device_id_type=MESH)
        c.start()
        smalls.append(c)

    for p in range(PIECES):
        seconds[p].wait()
        for i in range(p * n, (p + 1) * n):
            t = pair_out[i].astype(F32) + pair_in[i].astype(F32)
            gf[core, :, 2 * i * LN:(2 * i + 1) * LN] = t[0:8]
            gf[core, :, (2 * i + 1) * LN:(2 * i + 2) * LN] = t[8:16]
        part = gf.at[core, :, pl.ds(p * 2 * n * LN, 2 * n * LN)]
        c = pltpu.make_async_remote_copy(
            src_ref=part, dst_ref=part, send_sem=s2.at[4 + PIECES + p], recv_sem=r2.at[4 + PIECES + p],
            device_id={"dp": mate}, device_id_type=MESH)
        c.start()
        thirds.append(c)

    await_all(recvo, ro)
    for j in range(4):
        low = jnp.concatenate([recvo[16 * j + g].astype(F32)[0:8] for g in range(16)], 0)
        high = jnp.concatenate([recvo[16 * j + 15 - g].astype(F32)[8:16] for g in range(16)], 0)
        mixed[:, j * LN:(j + 1) * LN] = low.T.astype(BF)
        mixed[:, (7 - j) * LN:(8 - j) * LN] = high.T.astype(BF)

    for c in smalls:
        c.wait()
    total = (small_in[0] + small_in[1]) + (small_in[2] + small_in[3])
    row = lax.broadcasted_iota(jnp.int32, (CH, LN), 0)

    def flat_rows(item, target):
        return jnp.sum(jnp.where(row == target, total[:, item:item + 1], 0.0), 0, keepdims=True)[:, 0:8]
    for k in range(3):
        gs[0, k] = jnp.concatenate([flat_rows(k, lane), flat_rows(k, lane + 8)], 0)
        gs[1, k] = jnp.concatenate([
            flat_rows(3 + k, lane) + flat_rows(6 + k, 15 - lane),
            flat_rows(3 + k, 15 - lane) + flat_rows(6 + k, lane)], 0)
    await_all(sendx, sx)
    await_all(sendc, sc)
    await_all(sendo, so)
    for c in thirds:
        c.wait()


def write(a, b, c, a_h, b_h, c_h, sems):
    copies = [pltpu.make_async_copy(x, y, sems.at[i]) for i, (x, y) in enumerate(((b, b_h), (a, a_h), (c, c_h)))]
    for x in copies:
        x.start()
    for x in copies:
        x.wait()


def run_kernel(hid, cot, filt, sw):
    amat, bmat, tws, mats = constants()
    vm = pl.BlockSpec(memory_space=pltpu.VMEM)
    dma = pltpu.SemaphoreType.DMA
    chunks = pltpu.VMEM((NB, CH, LN), BF)
    flat = pltpu.VMEM((NB * CH, LN), F32)
    padded = pltpu.VMEM(((NB + 2) * CH, LN), F32)
    spec = pltpu.VMEM((CH * NB, 2 * LN), F32)
    ops = (hid, cot, filt, sw, jnp.asarray(amat), jnp.asarray(bmat), jnp.asarray(tws), jnp.asarray(mats))
    held = [pltpu.VMEM(a.shape, a.dtype) for a in ops]
    outs = pl.pallas_call(
        kernel,
        out_shape=(
            pltpu.VMEM((LN, 1024), BF),
            pltpu.VMEM((2, 8, NB * LN), F32),
            pltpu.VMEM((2, 3, 2, 8), F32),
        ),
        in_specs=[pl.BlockSpec(memory_space=pltpu.HBM)] * 8,
        out_specs=(vm,) * 3,
        scratch_shapes=held + [chunks] * 6 + [padded] * 2 + [pltpu.VMEM((2, (NB + 2) * 8, LN), F32)] + [flat] * 6 + [spec] * 5 + [
            pltpu.VMEM((2, CH * NB, 2 * LN), BF),
            pltpu.VMEM((2, CH * NB, 2 * LN), BF),
            pltpu.VMEM((NB // 2, CH, LN), F32),
            pltpu.VMEM((NB // 2, CH, LN), BF),
            pltpu.VMEM((NB // 2, CH, LN), BF),
            pltpu.VMEM((NB // 2, CH, LN), BF),
            pltpu.VMEM((NB // 2, CH, LN), BF),
            pltpu.VMEM((4, CH, LN), F32),
            dma, dma, dma, dma, dma, dma, dma((4 + 2 * PIECES,)), dma((4 + 2 * PIECES,)), dma((8,)),
        ],
        compiler_params=pltpu.CompilerParams(
            vmem_limit_bytes=57 << 20, collective_id=0, has_side_effects=True),
    )(*ops)
    return pl.pallas_call(
        write,
        out_shape=tuple(jax.ShapeDtypeStruct(a.shape, a.dtype) for a in outs),
        in_specs=[vm] * 3,
        out_specs=(pl.BlockSpec(memory_space=pltpu.HBM),) * 3,
        scratch_shapes=[dma((3,))],
        compiler_params=pltpu.CompilerParams(vmem_limit_bytes=1 << 20),
    )(*outs)


def local(hidden, sw, filt, cot):
    mixed, gf, gs = run_kernel(hidden[0], cot[0], filt, jnp.swapaxes(sw, 0, 1))
    return mixed[None], gf, gs


def solution(mesh):
    in_specs = (P("dp", "ctx", None), P(), P(None, "ctx", None), P("dp", "ctx", None))
    out_specs = (P("dp", "ctx", None), P(None, "ctx", None), P(None, None, None, "ctx"))
    return jax.shard_map(local, mesh=mesh, in_specs=in_specs, out_specs=out_specs, check_vma=False)
```
